512 devices in a mesh: ctx: 64 (over z, x), tp: 8 (over y, core).
Axes of the slice: x: 4, y: 4, z: 16, core: 2. Of those that a mesh axis runs over, the one named last changes fastest.
Arguments:
- tokens: bfloat16 [65536, 4096], P(('ctx', 'tp')), may hold values from -26 to 26
- query_weight: bfloat16 [4096, 2048], P('ctx', 'tp'), may hold values from -0.09375 to 0.09375
- kv_weight: bfloat16 [4096, 2048], P('ctx', 'tp'), may hold values from -0.09375 to 0.09375
- reach: int32 [1024], P('ctx'), may hold values from 1 to 2, as said below
- global_ids: int32 [2], replicated, may hold values from 0 to 1023, as said below
- rand_ids: int32 [1024, 3], replicated, may hold values from -1 to 1023, as said below
Outputs:
- attended: bfloat16 [65536, 2048], P('ctx', 'tp')
The draws below stay inside these ranges and needn't reach their ends.
Inputs may be any that keep to these rules, and one draw needn't show every extreme that they name: Some query block has reach 2. `global_ids`: distinct block numbers; the last entry is block 1023. `rand_ids`: the -1 entries of a query block come after its other entries; the 16 query blocks of a run (blocks 16 * i to 16 * i + 15) list at most 2 entries, repeats counted, that name blocks of any one run; in some run all entries are filled and some run of key blocks is named by exactly 2 of them.
All inputs are finite; a program needn't handle non-finite values.
Results may differ from the reference program's by a relative error of at most 0.012.
The reference program's roundings to bfloat16 on the way count: a program that leaves them out, or rounds other values in their place, can miss the bound.
Values may be sent and summed in bfloat16 or wider, within the bound.
No kernel may reach another device: no remote copies, remote signals or barrier semaphores. Data moves between devices by JAX's collectives and lax.ppermute only.
A program may use at most 64 MiB of HBM per device.

```python
import jax
import jax.numpy as jnp
from jax import lax

D = 4096
HEADS = 16
KV_HEADS = 8
HD = 128
GROUP = 2
BS = 64
WMAX = 2
G = 2
RMAX = 3
BPS = 16
NB = 1024
SEQ = 65536
CAP = 2
N_CTX = 64


def draw_tokens(key, part):
    values = jnp.clip(jax.random.normal(key, (SEQ, D), jnp.float32), -4.0, 4.0)
    return values.astype(jnp.bfloat16)


def draw_reach(key, part):
    values = jax.random.randint(key, (NB,), 1, WMAX + 1)
    spot = jax.random.randint(jax.random.fold_in(key, 7), (), 0, NB)
    return jnp.where(jnp.arange(NB) == spot, WMAX, values).astype(jnp.int32)


def draw_global_ids(key, part):
    key = jax.random.fold_in(key, 31)
    others = jax.random.permutation(key, NB - 1)[:G - 1]
    return jnp.concatenate([others, jnp.full((1,), NB - 1, jnp.int32)]).astype(jnp.int32)


def draw_rand_ids(key, part):
    slot_count = BPS * RMAX
    owners_each = (slot_count + CAP - 1) // CAP
    hot_key = jax.random.fold_in(key, 21)
    score_key = jax.random.fold_in(key, 22)
    perm_key = jax.random.fold_in(key, 23)
    pick_key = jax.random.fold_in(key, 24)
    count_key = jax.random.fold_in(key, 25)
    full_key = jax.random.fold_in(key, 26)
    boost = jnp.where(jax.random.randint(hot_key, (N_CTX,), 0, 8) == 0, 4096, 0)
    owner_scores = (jax.random.randint(score_key, (N_CTX, N_CTX), 0, 4096) + boost[None, :]) * N_CTX + jnp.arange(N_CTX)[None, :]
    chosen = lax.top_k(owner_scores, owners_each)[1]
    slot_order = jax.vmap(lambda sub_key: jax.random.permutation(sub_key, slot_count))(jax.random.split(perm_key, N_CTX))
    owner = jnp.take_along_axis(chosen, slot_order // CAP, axis=1)
    inside = jax.random.randint(pick_key, (N_CTX, slot_count), 0, BPS)
    listed = (owner * BPS + inside).reshape(NB, RMAX)
    counts = jax.random.randint(count_key, (NB,), 2, RMAX + 1)
    full_run = jax.random.randint(full_key, (), 0, N_CTX)
    counts = jnp.where(jnp.arange(NB) // BPS == full_run, RMAX, counts)
    return jnp.where(jnp.arange(RMAX)[None, :] < counts[:, None], listed, -1).astype(jnp.int32)


def block_scale(key, extent, cuts, low, high):
    def one(dim, blocks):
        draws = jax.random.uniform(jax.random.fold_in(jax.random.fold_in(key, 6), dim), (blocks,), jnp.float32, low / len(cuts), high / len(cuts))
        return jnp.repeat(jnp.exp(draws), extent[dim] // blocks).reshape((-1,) + (1,) * (len(extent) - dim - 1))

    gain = one(*cuts[0])
    for cut in cuts[1:]:
        gain = gain * one(*cut)
    return gain


def centred(rng, extent, deviation, limit, cuts=(), kind=jnp.bfloat16):
    drawn = deviation * jax.random.normal(rng, extent, jnp.float32)
    if cuts:
        drawn = drawn * block_scale(rng, extent, cuts, -0.22, 0.18)
    return jnp.clip(drawn, -limit, limit).astype(kind)


def setup_inputs(seed: int = 0) -> dict:
    arg_keys = jax.random.split(jax.random.key(seed), 7)
    tokens = draw_tokens(jax.random.fold_in(arg_keys[6], 71), 0)
    query_weight = centred(arg_keys[1], (D, HEADS * HD), D ** -0.5, 0.09375, ((0, 64), (1, 8)))
    kv_weight = centred(arg_keys[2], (D, 2 * KV_HEADS * HD), D ** -0.5, 0.09375, ((0, 64), (1, 8)))
    reach = draw_reach(jax.random.fold_in(arg_keys[6], 71), 0)
    global_ids = draw_global_ids(jax.random.fold_in(arg_keys[6], 71), 0)
    rand_ids = draw_rand_ids(jax.random.fold_in(arg_keys[6], 71), 0)
    return dict(tokens=tokens, query_weight=query_weight, kv_weight=kv_weight, reach=reach, global_ids=global_ids, rand_ids=rand_ids)


masked_score = -1.0e30


def attend_block(query_block, slabs, slot_valid):
    query_float = query_block.astype(jnp.float32)
    slab_float = slabs.astype(jnp.float32)
    slot_count = slabs.shape[0]
    scores = jnp.einsum("qkgd,sjkd->kgqsj", query_float, slab_float[:, :, :, 0, :])
    scores = scores.reshape(scores.shape[:3] + (slot_count * BS,)) * HD ** -0.5
    key_live = jnp.repeat(slot_valid, BS)
    scores = jnp.where(key_live[None, None, None, :], scores, masked_score)
    row_max = jnp.max(scores, axis=-1, keepdims=True)
    exponent = jnp.exp(scores - row_max)
    weights = (exponent / jnp.sum(exponent, axis=-1, keepdims=True)).astype(jnp.bfloat16)
    weights = weights.reshape(weights.shape[:3] + (slot_count, BS)).astype(jnp.float32)
    mixed = jnp.einsum("kgqsj,sjkd->qkgd", weights, slab_float[:, :, :, 1, :])
    return mixed.astype(jnp.bfloat16).reshape(BS, HEADS * HD)


def reference(tokens, query_weight, kv_weight, reach, global_ids, rand_ids):
    block_total = tokens.shape[0] // BS
    query_rows = jnp.dot(tokens, query_weight, preferred_element_type=jnp.float32).astype(jnp.bfloat16)
    key_rows = jnp.dot(tokens, kv_weight, preferred_element_type=jnp.float32).astype(jnp.bfloat16)
    query_blocks = query_rows.reshape(block_total, BS, KV_HEADS, GROUP, HD)
    key_blocks = key_rows.reshape(block_total, BS, KV_HEADS, 2, HD)
    offsets = jnp.arange(-WMAX, WMAX + 1).astype(jnp.int32)

    def one_block(block_id):
        target = block_id + offsets
        window_live = (jnp.abs(offsets) <= reach[block_id]) & (target >= 0) & (target < block_total)
        listed = rand_ids[block_id]
        slot_ids = jnp.concatenate([target, global_ids, listed]).astype(jnp.int32)
        slot_valid = jnp.concatenate([window_live, jnp.ones((G,), jnp.bool_), listed >= 0])
        slabs = key_blocks[jnp.clip(slot_ids, 0, block_total - 1)]
        return attend_block(query_blocks[block_id], slabs, slot_valid)

    def one_group(block_ids):
        return jax.vmap(one_block)(block_ids)

    groups = jnp.arange(block_total, dtype=jnp.int32).reshape(-1, 8)
    outputs = lax.map(one_group, groups)
    return outputs.reshape(block_total * BS, HEADS * HD)
```

```python
import functools

import jax
import jax.numpy as jnp
from jax import lax
from jax.experimental import pallas as pl
from jax.experimental.pallas import tpu as pltpu
from jax.sharding import Mesh, PartitionSpec as P

HD = 128
BS = 64
WMAX = 2
SLOTS = 10
CHUNK = 4
UNROLL = 4
SLOT_ROOM = 12
RUN_BLOCKS = 16
PAD = 16
LOG2E = 1.4426950408889634
MASKED = -1e30
F32 = jnp.float32
BF16 = jnp.bfloat16
NT = (((1,), (1,)), ((), ()))
TN = (((0,), (0,)), ((), ()))


def shift(value, axis, by):
    size = lax.axis_size(axis)
    return lax.ppermute(value, axis, [(i, (i + by) % size) for i in range(size)])


def project_kernel(place, rows, part0, part1, part2, part3, out, weight):
    @pl.when(pl.program_id(0) == 0)
    def _():
        for s, part in enumerate((part0, part1, part2, part3)):
            owner = lax.rem(place[0] + 4 - s, 4)
            for za in range(4):
                for zb in range(4):
                    weight[za * 4 + zb, owner] = part[zb, za]

    depth = rows.shape[1]
    flat = weight[...].reshape(depth, out.shape[1])
    out[...] = jnp.dot(rows[...], flat, preferred_element_type=F32).astype(BF16)


def project(place, rows, parts):
    count, depth = rows.shape
    width = parts[0].shape[-1]
    tile = 256
    whole = pl.BlockSpec(parts[0].shape, lambda i, p: (0, 0, 0, 0))
    return pl.pallas_call(
        project_kernel,
        grid_spec=pltpu.PrefetchScalarGridSpec(
            num_scalar_prefetch=1,
            grid=(count // tile,),
            in_specs=[pl.BlockSpec((tile, depth), lambda i, p: (i, 0))] + [whole] * 4,
            out_specs=pl.BlockSpec((tile, width), lambda i, p: (i, 0)),
            scratch_shapes=[pltpu.VMEM((16, 4, 64, width), BF16)],
        ),
        out_shape=jax.ShapeDtypeStruct((count, width), BF16),
        compiler_params=pltpu.CompilerParams(vmem_limit_bytes=40 << 20),
        cost_estimate=pl.CostEstimate(
            flops=2 * count * depth * width,
            bytes_accessed=2 * (count * depth + depth * width + count * width),
            transcendentals=0,
        ),
        name="project",
    )(place, rows, *parts)


def partial_kernel(from_x, index, counts, query, held, out, slabs, sems):
    base = from_x[0] * RUN_BLOCKS

    def copy(j, p):
        block = index[(base + j) * SLOTS + p]
        return pltpu.make_async_copy(
            held.at[block], slabs.at[j, pl.ds(p * BS, BS)], sems.at[j, p]
        )

    def start_block(j, carry):
        def start(p, inner):
            copy(j, p).start()
            return inner

        return lax.fori_loop(0, counts[base + j], start, carry)

    lax.fori_loop(0, RUN_BLOCKS, start_block, 0)

    def group(g, carry):
        first = g * UNROLL
        live = [counts[base + first + u] for u in range(UNROLL)]

        for u in range(UNROLL):

            def wait(p, inner, u=u):
                copy(first + u, p).wait()
                return inner

            lax.fori_loop(0, live[u], wait, 0)

        most = functools.reduce(jnp.maximum, live)
        row0 = g * (UNROLL * BS + PAD)

        def attend(chunks):
            keys = chunks * CHUNK * BS
            line = lax.broadcasted_iota(jnp.int32, (keys, HD), 0)
            spot = lax.broadcasted_iota(jnp.int32, (PAD, HD), 0)
            stats = jnp.zeros((PAD, HD), F32)
            for u in range(UNROLL):
                q_rows = query[pl.ds((first + u) * BS, BS), :]
                q_both = jnp.concatenate([q_rows[:, :HD], q_rows[:, HD:]], axis=0)
                key = slabs[first + u, 0:keys, 0:HD]
                value = slabs[first + u, 0:keys, HD : 2 * HD]
                inside = line < live[u] * BS
                value = jnp.where(inside, value, jnp.zeros_like(value))
                scores = lax.dot_general(key, q_both, NT, preferred_element_type=F32)
                scores = jnp.where(inside, scores * (HD**-0.5 * LOG2E), MASKED)
                top = jnp.max(scores, axis=0, keepdims=True)
                power = jnp.where(inside, jnp.exp2(scores - top), 0.0)
                total = jnp.sum(power, axis=0, keepdims=True)
                some = total > 0.0
                total = jnp.where(some, total, 1.0)
                weights = (power * (1.0 / total)).astype(BF16)
                mixed = lax.dot_general(weights, value, TN, preferred_element_type=F32)
                mixed = mixed.astype(BF16)
                out[pl.ds(row0 + u * BS, BS), 0:HD] = mixed[:BS]
                out[pl.ds(row0 + u * BS, BS), HD : 2 * HD] = mixed[BS:]
                level = jnp.where(some, top + jnp.log2(total), MASKED)
                high = level.astype(BF16).astype(F32)
                middle = (level - high).astype(BF16).astype(F32)
                low = level - high - middle
                for t, piece in enumerate((high, middle, low)):
                    stats = jnp.where(spot == 3 * u + t, piece, stats)
            out[pl.ds(row0 + UNROLL * BS, PAD), 0:HD] = stats.astype(BF16)
            out[pl.ds(row0 + UNROLL * BS, PAD), HD : 2 * HD] = jnp.zeros((PAD, HD), BF16)

        for chunks in (1, 2, 3):
            low_edge = (chunks - 1) * CHUNK if chunks > 1 else -1

            @pl.when((most > low_edge) & (most <= chunks * CHUNK))
            def _(chunks=chunks):
                attend(chunks)

        return carry

    lax.fori_loop(0, RUN_BLOCKS // UNROLL, group, 0)


def partial_attention(from_x, index, counts, query, held):
    rows = RUN_BLOCKS // UNROLL * (UNROLL * BS + PAD)
    smem = pl.BlockSpec(memory_space=pltpu.SMEM)
    vmem = pl.BlockSpec(memory_space=pltpu.VMEM)
    return pl.pallas_call(
        partial_kernel,
        in_specs=[smem, smem, smem, vmem, pl.BlockSpec(memory_space=pl.ANY)],
        out_specs=vmem,
        out_shape=jax.ShapeDtypeStruct((rows, 2 * HD), BF16),
        scratch_shapes=[
            pltpu.VMEM((RUN_BLOCKS, SLOT_ROOM * BS, 2 * HD), BF16),
            pltpu.SemaphoreType.DMA((RUN_BLOCKS, SLOTS)),
        ],
        compiler_params=pltpu.CompilerParams(vmem_limit_bytes=40 << 20),
        cost_estimate=pl.CostEstimate(
            flops=10 * 10**9, bytes_accessed=4 << 20, transcendentals=0
        ),
        name="partial_attention",
    )(from_x, index, counts, query, held)


def combine_kernel(part0, part1, part2, part3, out):
    parts = (part0, part1, part2, part3)
    spot = lax.broadcasted_iota(jnp.int32, (HD, HD), 0)
    tail = [part[pl.ds(UNROLL * BS, PAD), 0:HD].astype(F32) for part in parts]
    for u in range(UNROLL):
        levels = [
            t[3 * u : 3 * u + 1] + t[3 * u + 1 : 3 * u + 2] + t[3 * u + 2 : 3 * u + 3]
            for t in tail
        ]
        top = functools.reduce(jnp.maximum, levels)
        shares = [jnp.exp2(level - top) for level in levels]
        norm = 1.0 / functools.reduce(jnp.add, shares)
        table = jnp.zeros((HD, HD), F32)
        for k, share in enumerate(shares):
            table = jnp.where(spot == k, share * norm, table)
        table = table.T
        for h in range(2):
            lanes = slice(h * HD, (h + 1) * HD)
            mixed = jnp.zeros((BS, HD), F32)
            for k, part in enumerate(parts):
                scale = table[h * BS : (h + 1) * BS, k : k + 1]
                mixed += scale * part[u * BS : (u + 1) * BS, lanes].astype(F32)
            out[u * BS : (u + 1) * BS, lanes] = mixed.astype(BF16)


def combine(parts):
    groups = RUN_BLOCKS // UNROLL
    spec = pl.BlockSpec((UNROLL * BS + PAD, 2 * HD), lambda i: (i, 0))
    return pl.pallas_call(
        combine_kernel,
        grid=(groups,),
        in_specs=[spec] * 4,
        out_specs=pl.BlockSpec((UNROLL * BS, 2 * HD), lambda i: (i, 0)),
        out_shape=jax.ShapeDtypeStruct((RUN_BLOCKS * BS, 2 * HD), BF16),
        name="combine",
    )(*parts)


def slot_lists(reach_plane, global_ids, rand_ids, plane, place):
    plane_blocks = 4 * RUN_BLOCKS
    block_total = rand_ids.shape[0]
    first = plane * plane_blocks
    blocks = first + jnp.arange(plane_blocks, dtype=jnp.int32)
    offsets = jnp.arange(-WMAX, WMAX + 1, dtype=jnp.int32)
    target = blocks[:, None] + offsets[None, :]
    window_live = (
        (jnp.abs(offsets)[None, :] <= reach_plane[:, None])
        & (target >= 0)
        & (target < block_total)
    )
    listed = lax.dynamic_slice_in_dim(rand_ids, first, plane_blocks, 0)
    globals_all = jnp.broadcast_to(global_ids[None, :], (plane_blocks, global_ids.shape[0]))
    slots = jnp.concatenate([target, globals_all, listed], axis=1)
    live = jnp.concatenate(
        [window_live, jnp.ones(globals_all.shape, jnp.bool_), listed >= 0], axis=1
    )
    held = live & ((slots >> 4) % 4 == place)
    local = (slots >> 6) * RUN_BLOCKS + (slots & (RUN_BLOCKS - 1))
    order = jnp.arange(SLOTS)
    before = order[:, None] < order[None, :]
    rank = jnp.sum(jnp.where(held[:, :, None] & before[None], 1, 0), axis=1)
    at = held[:, :, None] & (rank[:, :, None] == order[None, None, :])
    index = jnp.sum(jnp.where(at, local[:, :, None], 0), axis=1)
    counts = jnp.sum(held.astype(jnp.int32), axis=1)
    return index.reshape(-1).astype(jnp.int32), counts.astype(jnp.int32)


def per_device(tokens, query_weight, kv_weight, reach, global_ids, rand_ids):
    place = lax.axis_index("x").astype(jnp.int32)
    plane = (lax.axis_index("a") * 4 + lax.axis_index("b")).astype(jnp.int32)
    width = query_weight.shape[1]

    rows = lax.all_gather(tokens, ("y", "c"), axis=0, tiled=True)

    both = jnp.concatenate([kv_weight, query_weight], axis=1)
    both = lax.all_gather(both, "a", axis=0, tiled=True)
    kv_own = lax.all_gather(both[:, :width], "b", axis=0, tiled=True)
    query_own_in, kv_own = lax.optimization_barrier((both[:, width:], kv_own))
    query_own = lax.all_gather(query_own_in, "b", axis=0, tiled=True)

    def spread(own):
        own = own.reshape(4, 4, 64, width)
        return [own] + [shift(own, "x", s) for s in (1, 2, 3)]

    place_1 = place.reshape(1)
    kv_rows = project(place_1, rows, spread(kv_own))
    held = lax.all_gather(kv_rows, ("a", "b"), axis=0, tiled=True)
    held = held.reshape(-1, BS, 2 * HD)
    query_rows = project(place_1, rows, spread(query_own))
    queries = [query_rows] + [shift(query_rows, "x", s) for s in (1, 2, 3)]

    reach_plane = lax.all_gather(reach, "x", axis=0, tiled=True)
    index, counts = slot_lists(reach_plane, global_ids, rand_ids, plane, place)

    parts = [None] * 4
    for s in (2, 1, 3, 0):
        from_x = ((place + 4 - s) % 4).reshape(1)
        part = partial_attention(from_x, index, counts, queries[s], held)
        parts[s] = part if s == 0 else shift(part, "x", 4 - s)
    return combine(parts)


def solution(mesh):
    inner = Mesh(mesh.devices.reshape(4, 4, 4, 4, 2), ("a", "b", "x", "y", "c"))
    ctx, tp = ("a", "b", "x"), ("y", "c")
    in_specs = (P(ctx + tp, None), P(ctx, tp), P(ctx, tp), P(ctx), P(), P())
    return jax.shard_map(
        per_device, mesh=inner, in_specs=in_specs, out_specs=P(ctx, tp), check_vma=False
    )
```

```python
import functools

import jax
import jax.numpy as jnp
from jax import lax
from jax.experimental import pallas as pl
from jax.experimental.pallas import tpu as pltpu
from jax.sharding import Mesh, PartitionSpec as P

HD = 128
BS = 64
WMAX = 2
CHUNK = 2
UNROLL = 4
SLOT_ROOM = 8
RUN_BLOCKS = 16
PAD = 16
LOG2E = 1.4426950408889634
MASKED = -1e30
F32 = jnp.float32
BF16 = jnp.bfloat16
NT = (((1,), (1,)), ((), ()))
TN = (((0,), (0,)), ((), ()))


def shift(value, axis, by):
    size = lax.axis_size(axis)
    return lax.ppermute(value, axis, [(i, (i + by) % size) for i in range(size)])


def project_kernel(place, rows, part0, part1, part2, part3, out, weight):
    @pl.when(pl.program_id(0) == 0)
    def _():
        for s, part in enumerate((part0, part1, part2, part3)):
            owner = lax.rem(place[0] + 4 - s, 4)
            for za in range(4):
                for zb in range(4):
                    weight[za * 4 + zb, owner] = part[zb, za]

    depth = rows.shape[1]
    flat = weight[...].reshape(depth, out.shape[1])
    out[...] = jnp.dot(rows[...], flat, preferred_element_type=F32).astype(BF16)


def project(place, rows, parts):
    count, depth = rows.shape
    width = parts[0].shape[-1]
    tile = 256
    whole = pl.BlockSpec(parts[0].shape, lambda i, p: (0, 0, 0, 0))
    return pl.pallas_call(
        project_kernel,
        grid_spec=pltpu.PrefetchScalarGridSpec(
            num_scalar_prefetch=1,
            grid=(count // tile,),
            in_specs=[pl.BlockSpec((tile, depth), lambda i, p: (i, 0))] + [whole] * 4,
            out_specs=pl.BlockSpec((tile, width), lambda i, p: (i, 0)),
            scratch_shapes=[pltpu.VMEM((16, 4, 64, width), BF16)],
        ),
        out_shape=jax.ShapeDtypeStruct((count, width), BF16),
        compiler_params=pltpu.CompilerParams(vmem_limit_bytes=50 << 20),
        cost_estimate=pl.CostEstimate(
            flops=2 * count * depth * width,
            bytes_accessed=2 * (count * depth + depth * width + count * width),
            transcendentals=0,
        ),
        name="project",
    )(place, rows, *parts)


def partial_kernel(from_x, index, counts, query, held, out, slabs, sems):
    base = from_x[0] * RUN_BLOCKS

    def copy(j, p):
        block = index[(base + j) * SLOT_ROOM + p]
        return pltpu.make_async_copy(
            held.at[block], slabs.at[j, pl.ds(p * BS, BS)], sems.at[j, p]
        )

    def start_block(j, carry):
        def start(p, inner):
            copy(j, p).start()
            return inner

        return lax.fori_loop(0, counts[base + j], start, carry)

    lax.fori_loop(0, RUN_BLOCKS, start_block, 0)

    def group(g, carry):
        first = g * UNROLL
        live = [counts[base + first + u] for u in range(UNROLL)]

        for u in range(UNROLL):

            def wait(p, inner, u=u):
                copy(first + u, p).wait()
                return inner

            lax.fori_loop(0, live[u], wait, 0)

        most = functools.reduce(jnp.maximum, live)
        row0 = g * (UNROLL * BS + PAD)

        def attend(chunks):
            keys = chunks * CHUNK * BS
            line = lax.broadcasted_iota(jnp.int32, (keys, HD), 0)
            spot = lax.broadcasted_iota(jnp.int32, (PAD, HD), 0)
            stats = jnp.zeros((PAD, HD), F32)
            for u in range(UNROLL):
                q_rows = query[pl.ds((first + u) * BS, BS), :]
                q_both = jnp.concatenate([q_rows[:, :HD], q_rows[:, HD:]], axis=0)
                key = slabs[first + u, 0:keys, 0:HD]
                value = slabs[first + u, 0:keys, HD : 2 * HD]
                inside = line < live[u] * BS
                value = jnp.where(inside, value, jnp.zeros_like(value))
                scores = lax.dot_general(key, q_both, NT, preferred_element_type=F32)
                scores = jnp.where(inside, scores * (HD**-0.5 * LOG2E), MASKED)
                top = jnp.max(scores, axis=0, keepdims=True)
                power = jnp.where(inside, jnp.exp2(scores - top), 0.0)
                total = jnp.sum(power, axis=0, keepdims=True)
                some = total > 0.0
                total = jnp.where(some, total, 1.0)
                weights = (power * (1.0 / total)).astype(BF16)
                mixed = lax.dot_general(weights, value, TN, preferred_element_type=F32)
                mixed = mixed.astype(BF16)
                out[pl.ds(row0 + u * BS, BS), 0:HD] = mixed[:BS]
                out[pl.ds(row0 + u * BS, BS), HD : 2 * HD] = mixed[BS:]
                level = jnp.where(some, top + jnp.log2(total), MASKED)
                high = level.astype(BF16).astype(F32)
                middle = (level - high).astype(BF16).astype(F32)
                low = level - high - middle
                for t, piece in enumerate((high, middle, low)):
                    stats = jnp.where(spot == 3 * u + t, piece, stats)
            out[pl.ds(row0 + UNROLL * BS, PAD), 0:HD] = stats.astype(BF16)
            out[pl.ds(row0 + UNROLL * BS, PAD), HD : 2 * HD] = jnp.zeros((PAD, HD), BF16)

        for chunks in (1, 2, 3, 4):
            low_edge = (chunks - 1) * CHUNK if chunks > 1 else -1

            @pl.when((most > low_edge) & (most <= chunks * CHUNK))
            def _(chunks=chunks):
                attend(chunks)

        return carry

    lax.fori_loop(0, RUN_BLOCKS // UNROLL, group, 0)


def partial_attention(from_x, index, counts, query, held):
    rows = RUN_BLOCKS // UNROLL * (UNROLL * BS + PAD)
    smem = pl.BlockSpec(memory_space=pltpu.SMEM)
    vmem = pl.BlockSpec(memory_space=pltpu.VMEM)
    return pl.pallas_call(
        partial_kernel,
        in_specs=[smem, smem, smem, vmem, pl.BlockSpec(memory_space=pl.ANY)],
        out_specs=vmem,
        out_shape=jax.ShapeDtypeStruct((rows, 2 * HD), BF16),
        scratch_shapes=[
            pltpu.VMEM((RUN_BLOCKS, SLOT_ROOM * BS, 2 * HD), BF16),
            pltpu.SemaphoreType.DMA((RUN_BLOCKS, SLOT_ROOM)),
        ],
        compiler_params=pltpu.CompilerParams(vmem_limit_bytes=50 << 20),
        cost_estimate=pl.CostEstimate(
            flops=10 * 10**9, bytes_accessed=4 << 20, transcendentals=0
        ),
        name="partial_attention",
    )(from_x, index, counts, query, held)


def combine_kernel(*refs):
    parts, out = refs[:-1], refs[-1]
    spot = lax.broadcasted_iota(jnp.int32, (HD, HD), 0)

    def group(g, carry):
        row0 = g * (UNROLL * BS + PAD)
        tail = [p[pl.ds(row0 + UNROLL * BS, PAD), 0:HD].astype(F32) for p in parts]
        for u in range(UNROLL):
            levels = [
                t[3 * u : 3 * u + 1] + t[3 * u + 1 : 3 * u + 2] + t[3 * u + 2 : 3 * u + 3]
                for t in tail
            ]
            top = functools.reduce(jnp.maximum, levels)
            shares = [jnp.exp2(level - top) for level in levels]
            norm = 1.0 / functools.reduce(jnp.add, shares)
            table = jnp.zeros((HD, HD), F32)
            for k, share in enumerate(shares):
                table = jnp.where(spot == k, share * norm, table)
            table = table.T
            for h in range(2):
                lanes = slice(h * HD, (h + 1) * HD)
                mixed = jnp.zeros((BS, HD), F32)
                for k, part in enumerate(parts):
                    scale = table[h * BS : (h + 1) * BS, k : k + 1]
                    mixed += scale * part[pl.ds(row0 + u * BS, BS), lanes].astype(F32)
                out[pl.ds((g * UNROLL + u) * BS, BS), lanes] = mixed.astype(BF16)
        return carry

    lax.fori_loop(0, RUN_BLOCKS // UNROLL, group, 0)


def combine(parts):
    vmem = pl.BlockSpec(memory_space=pltpu.VMEM)
    return pl.pallas_call(
        combine_kernel,
        in_specs=[vmem] * len(parts),
        out_specs=vmem,
        out_shape=jax.ShapeDtypeStruct((RUN_BLOCKS * BS, 2 * HD), BF16),
        compiler_params=pltpu.CompilerParams(vmem_limit_bytes=16 << 20),
        name="combine",
    )(*parts)


def pack(held, local):
    slots = held.shape[1]
    source, target = jnp.arange(slots), jnp.arange(SLOT_ROOM)
    before = source[:, None] < source[None, :]
    rank = jnp.sum(jnp.where(held[:, :, None] & before[None], 1, 0), axis=1)
    at = held[:, :, None] & (rank[:, :, None] == target[None, None, :])
    index = jnp.sum(jnp.where(at, local[:, :, None], 0), axis=1)
    counts = jnp.sum(held.astype(jnp.int32), axis=1)
    return index.reshape(-1).astype(jnp.int32), counts.astype(jnp.int32)


def own_lists(reach):
    offsets = jnp.arange(-WMAX, WMAX + 1, dtype=jnp.int32)
    target = jnp.arange(RUN_BLOCKS, dtype=jnp.int32)[:, None] + offsets[None, :]
    live = (
        (jnp.abs(offsets)[None, :] <= reach[:, None]) & (target >= 0) & (target < RUN_BLOCKS)
    )
    return pack(live, target)


def plane_lists(before, after, global_ids, rand_ids, plane, place):
    plane_blocks = 4 * RUN_BLOCKS
    block_total = rand_ids.shape[0]
    first = plane * plane_blocks
    blocks = jnp.arange(plane_blocks, dtype=jnp.int32)
    run = blocks // RUN_BLOCKS
    offsets = jnp.asarray([-2, -1, 1, 2], jnp.int32)
    target = first + blocks[:, None] + offsets[None, :]
    reach = jnp.where(
        (run == (place + 3) % 4)[:, None],
        jnp.tile(before, 4)[:, None],
        jnp.tile(after, 4)[:, None],
    )
    window_live = (
        (jnp.abs(offsets)[None, :] <= reach)
        & (target >= 0)
        & (target < block_total)
        & (target // RUN_BLOCKS != (first + blocks)[:, None] // RUN_BLOCKS)
    )
    listed = lax.dynamic_slice_in_dim(rand_ids, first, plane_blocks, 0)
    globals_all = jnp.broadcast_to(global_ids[None, :], (plane_blocks, global_ids.shape[0]))
    slots = jnp.concatenate([target, globals_all, listed], axis=1)
    live = jnp.concatenate(
        [window_live, jnp.ones(globals_all.shape, jnp.bool_), listed >= 0], axis=1
    )
    held = live & ((slots >> 4) % 4 == place)
    return pack(held, (slots >> 6) * RUN_BLOCKS + (slots & (RUN_BLOCKS - 1)))


def per_device(tokens, query_weight, kv_weight, reach, global_ids, rand_ids):
    place = lax.axis_index("x").astype(jnp.int32)
    plane = (lax.axis_index("a") * 4 + lax.axis_index("b")).astype(jnp.int32)
    width = query_weight.shape[1]

    rows = lax.all_gather(tokens, ("y", "c"), axis=0, tiled=True)

    both = jnp.concatenate([kv_weight, query_weight], axis=1)
    both = lax.all_gather(both, "a", axis=0, tiled=True)
    kv_own = lax.all_gather(both[:, :width], "b", axis=0, tiled=True)
    query_own_in, kv_own = lax.optimization_barrier((both[:, width:], kv_own))

    def spread(own):
        own = own.reshape(4, 4, 64, width)
        return [own] + [shift(own, "x", s) for s in (1, 2, 3)]

    kv_parts = spread(kv_own)
    query_own = lax.all_gather(query_own_in, "b", axis=0, tiled=True)
    kv_parts, query_own = lax.optimization_barrier((kv_parts, query_own))

    place_1 = place.reshape(1)
    kv_rows = project(place_1, rows, kv_parts)
    held = lax.all_gather(kv_rows, ("a", "b"), axis=0, tiled=True)
    held = held.reshape(-1, BS, 2 * HD)
    query_own, reach, kv_rows = lax.optimization_barrier((query_own, reach, kv_rows))
    query_rows = project(place_1, rows, spread(query_own))
    queries = [query_rows] + [shift(query_rows, "x", s) for s in (1, 2, 3)]

    own_index, own_counts = own_lists(reach)
    zero = jnp.zeros((1,), jnp.int32)
    own_held = kv_rows.reshape(-1, BS, 2 * HD)
    windows = partial_attention(zero, own_index, own_counts, query_rows, own_held)

    before, after = shift(reach, "x", 1), shift(reach, "x", 3)
    index, counts = plane_lists(before, after, global_ids, rand_ids, plane, place)
    held, windows, index, counts, queries = lax.optimization_barrier(
        (held, windows, index, counts, queries)
    )

    parts = [None] * 4
    for s in (2, 1, 3, 0):
        from_x = ((place + 4 - s) % 4).reshape(1)
        part = partial_attention(from_x, index, counts, queries[s], held)
        parts[s] = part if s == 0 else shift(part, "x", 4 - s)
    return combine(parts + [windows])


def solution(mesh):
    inner = Mesh(mesh.devices.reshape(4, 4, 4, 4, 2), ("a", "b", "x", "y", "c"))
    ctx, tp = ("a", "b", "x"), ("y", "c")
    in_specs = (P(ctx + tp, None), P(ctx, tp), P(ctx, tp), P(ctx), P(), P())
    return jax.shard_map(
        per_device, mesh=inner, in_specs=in_specs, out_specs=P(ctx, tp), check_vma=False
    )
```

```python
import functools

import jax
import jax.numpy as jnp
from jax import lax
from jax.experimental import pallas as pl
from jax.experimental.pallas import tpu as pltpu
from jax.sharding import Mesh, PartitionSpec as P

HD = 128
BS = 64
WMAX = 2
CHUNK = 2
UNROLL = 8
SLOT_ROOM = 8
RUN_BLOCKS = 16
PAD = 32
LOG2E = 1.4426950408889634
MASKED = -1e30
F32 = jnp.float32
BF16 = jnp.bfloat16
NT = (((1,), (1,)), ((), ()))
TN = (((0,), (0,)), ((), ()))


def shift(value, axis, by):
    size = lax.axis_size(axis)
    return lax.ppermute(value, axis, [(i, (i + by) % size) for i in range(size)])


def project_kernel(place, rows, part0, part1, part2, part3, out, weight):
    @pl.when(pl.program_id(0) == 0)
    def _():
        for s, part in enumerate((part0, part1, part2, part3)):
            owner = lax.rem(place[0] + 4 - s, 4)
            for za in range(4):
                for zb in range(4):
                    weight[za * 4 + zb, owner] = part[zb, za]

    depth = rows.shape[1]
    flat = weight[...].reshape(depth, out.shape[1])
    out[...] = jnp.dot(rows[...], flat, preferred_element_type=F32).astype(BF16)


def project(place, rows, parts):
    count, depth = rows.shape
    width = parts[0].shape[-1]
    tile = 512
    whole = pl.BlockSpec(memory_space=pltpu.VMEM)
    return pl.pallas_call(
        project_kernel,
        grid_spec=pltpu.PrefetchScalarGridSpec(
            num_scalar_prefetch=1,
            grid=(count // tile,),
            in_specs=[pl.BlockSpec((tile, depth), lambda i, p: (i, 0))] + [whole] * 4,
            out_specs=pl.BlockSpec((tile, width), lambda i, p: (i, 0)),
            scratch_shapes=[pltpu.VMEM((16, 4, 64, width), BF16)],
        ),
        out_shape=jax.ShapeDtypeStruct((count, width), BF16),
        compiler_params=pltpu.CompilerParams(vmem_limit_bytes=50 << 20),
        cost_estimate=pl.CostEstimate(
            flops=2 * count * depth * width,
            bytes_accessed=2 * (count * depth + depth * width + count * width),
            transcendentals=0,
        ),
        name="project",
    )(place, rows, *parts)


def partial_kernel(runs, from_x, index, counts, *refs):
    queries, held, outs = refs[:runs], refs[runs], refs[runs + 1 : 2 * runs + 1]
    slabs, sems = refs[-2:]

    def copy(r, j, p):
        row = (from_x[r] * RUN_BLOCKS + j) * SLOT_ROOM + p
        return pltpu.make_async_copy(
            held.at[index[row]],
            slabs.at[r * RUN_BLOCKS + j, pl.ds(p * BS, BS)],
            sems.at[r * RUN_BLOCKS + j, p],
        )

    for r in range(runs):

        def start_block(j, carry, r=r):
            def start(p, inner):
                copy(r, j, p).start()
                return inner

            return lax.fori_loop(0, counts[from_x[r] * RUN_BLOCKS + j], start, carry)

        lax.fori_loop(0, RUN_BLOCKS, start_block, 0)

    for r in range(runs):
        attend_run(r, from_x[r] * RUN_BLOCKS, counts, copy, queries[r], slabs, outs[r])


def attend_run(r, base, counts, copy, query, slabs, out):
    def group(g, carry):
        first = g * UNROLL
        live = [counts[base + first + u] for u in range(UNROLL)]

        for u in range(UNROLL):

            def wait(p, inner, u=u):
                copy(r, first + u, p).wait()
                return inner

            lax.fori_loop(0, live[u], wait, 0)

        most = functools.reduce(jnp.maximum, live)
        row0 = g * (UNROLL * BS + PAD)

        def attend(chunks):
            keys = chunks * CHUNK * BS
            line = lax.broadcasted_iota(jnp.int32, (keys, HD), 0)
            spot = lax.broadcasted_iota(jnp.int32, (PAD, HD), 0)
            each = range(UNROLL)
            inside = [line < live[u] * BS for u in each]
            scores = []
            for u in each:
                q_rows = query[pl.ds((first + u) * BS, BS), :]
                q_both = jnp.concatenate([q_rows[:, :HD], q_rows[:, HD:]], axis=0)
                key = slabs[r * RUN_BLOCKS + first + u, 0:keys, 0:HD]
                scores.append(lax.dot_general(key, q_both, NT, preferred_element_type=F32))
            scores = [
                jnp.where(inside[u], scores[u] * (HD**-0.5 * LOG2E), MASKED) for u in each
            ]
            tops = [jnp.max(scores[u], axis=0, keepdims=True) for u in each]
            powers = [
                jnp.where(inside[u], jnp.exp2(scores[u] - tops[u]), 0.0) for u in each
            ]
            totals = [jnp.sum(powers[u], axis=0, keepdims=True) for u in each]
            some = [totals[u] > 0.0 for u in each]
            totals = [jnp.where(some[u], totals[u], 1.0) for u in each]
            weights = [(powers[u] * (1.0 / totals[u])).astype(BF16) for u in each]
            mixes = []
            for u in each:
                value = slabs[r * RUN_BLOCKS + first + u, 0:keys, HD : 2 * HD]
                value = jnp.where(inside[u], value, jnp.zeros_like(value))
                mixes.append(
                    lax.dot_general(weights[u], value, TN, preferred_element_type=F32)
                )
            stats = jnp.zeros((PAD, HD), F32)
            for u in each:
                level = jnp.where(some[u], tops[u] + jnp.log2(totals[u]), MASKED)
                high = level.astype(BF16).astype(F32)
                middle = (level - high).astype(BF16).astype(F32)
                for t, piece in enumerate((high, middle, level - high - middle)):
                    stats = jnp.where(spot == 3 * u + t, piece, stats)
            for u in each:
                mixed = mixes[u].astype(BF16)
                out[pl.ds(row0 + u * BS, BS), 0:HD] = mixed[:BS]
                out[pl.ds(row0 + u * BS, BS), HD : 2 * HD] = mixed[BS:]
            out[pl.ds(row0 + UNROLL * BS, PAD), 0:HD] = stats.astype(BF16)
            out[pl.ds(row0 + UNROLL * BS, PAD), HD : 2 * HD] = jnp.zeros((PAD, HD), BF16)

        for chunks in (1, 2, 3, 4):
            low_edge = (chunks - 1) * CHUNK if chunks > 1 else -1

            @pl.when((most > low_edge) & (most <= chunks * CHUNK))
            def _(chunks=chunks):
                attend(chunks)

        return carry

    lax.fori_loop(0, RUN_BLOCKS // UNROLL, group, 0)


def partial_attention(from_x, index, counts, queries, held):
    runs = len(queries)
    rows = RUN_BLOCKS // UNROLL * (UNROLL * BS + PAD)
    smem = pl.BlockSpec(memory_space=pltpu.SMEM)
    vmem = pl.BlockSpec(memory_space=pltpu.VMEM)
    return pl.pallas_call(
        functools.partial(partial_kernel, runs),
        in_specs=[smem] * 3 + [vmem] * runs + [pl.BlockSpec(memory_space=pl.ANY)],
        out_specs=[vmem] * runs,
        out_shape=[jax.ShapeDtypeStruct((rows, 2 * HD), BF16)] * runs,
        scratch_shapes=[
            pltpu.VMEM((runs * RUN_BLOCKS, SLOT_ROOM * BS, 2 * HD), BF16),
            pltpu.SemaphoreType.DMA((runs * RUN_BLOCKS, SLOT_ROOM)),
        ],
        compiler_params=pltpu.CompilerParams(vmem_limit_bytes=50 << 20),
        cost_estimate=pl.CostEstimate(
            flops=runs * 5 * 10**9, bytes_accessed=4 << 20, transcendentals=0
        ),
        name="partial_attention",
    )(from_x, index, counts, *queries, held)


def combine_kernel(*refs):
    parts, out = refs[:-1], refs[-1]
    spot = lax.broadcasted_iota(jnp.int32, (HD, HD), 0)

    def group(g, carry):
        row0 = g * (UNROLL * BS + PAD)
        tail = [p[pl.ds(row0 + UNROLL * BS, PAD), 0:HD].astype(F32) for p in parts]
        tables = []
        for u in range(UNROLL):
            levels = [
                t[3 * u : 3 * u + 1] + t[3 * u + 1 : 3 * u + 2] + t[3 * u + 2 : 3 * u + 3]
                for t in tail
            ]
            top = functools.reduce(jnp.maximum, levels)
            shares = [jnp.exp2(level - top) for level in levels]
            norm = 1.0 / functools.reduce(jnp.add, shares)
            table = jnp.zeros((HD, HD), F32)
            for k, share in enumerate(shares):
                table = jnp.where(spot == k, share * norm, table)
            tables.append(table.T)
        for u in range(UNROLL):
            for h in range(2):
                lanes = slice(h * HD, (h + 1) * HD)
                mixed = jnp.zeros((BS, HD), F32)
                for k, part in enumerate(parts):
                    scale = tables[u][h * BS : (h + 1) * BS, k : k + 1]
                    mixed += scale * part[pl.ds(row0 + u * BS, BS), lanes].astype(F32)
                out[pl.ds((g * UNROLL + u) * BS, BS), lanes] = mixed.astype(BF16)
        return carry

    lax.fori_loop(0, RUN_BLOCKS // UNROLL, group, 0)


def combine(parts):
    vmem = pl.BlockSpec(memory_space=pltpu.VMEM)
    return pl.pallas_call(
        combine_kernel,
        in_specs=[vmem] * len(parts),
        out_specs=vmem,
        out_shape=jax.ShapeDtypeStruct((RUN_BLOCKS * BS, 2 * HD), BF16),
        compiler_params=pltpu.CompilerParams(vmem_limit_bytes=16 << 20),
        name="combine",
    )(*parts)


def pack(held, local):
    slots = held.shape[1]
    source, target = jnp.arange(slots), jnp.arange(SLOT_ROOM)
    before = source[:, None] < source[None, :]
    rank = jnp.sum(jnp.where(held[:, :, None] & before[None], 1, 0), axis=1)
    at = held[:, :, None] & (rank[:, :, None] == target[None, None, :])
    index = jnp.sum(jnp.where(at, local[:, :, None], 0), axis=1)
    counts = jnp.sum(held.astype(jnp.int32), axis=1)
    return index.reshape(-1).astype(jnp.int32), counts.astype(jnp.int32)


def own_lists(reach):
    offsets = jnp.arange(-WMAX, WMAX + 1, dtype=jnp.int32)
    target = jnp.arange(RUN_BLOCKS, dtype=jnp.int32)[:, None] + offsets[None, :]
    live = (
        (jnp.abs(offsets)[None, :] <= reach[:, None]) & (target >= 0) & (target < RUN_BLOCKS)
    )
    return pack(live, target)


def plane_lists(before, after, global_ids, rand_ids, plane, place):
    plane_blocks = 4 * RUN_BLOCKS
    block_total = rand_ids.shape[0]
    first = plane * plane_blocks
    blocks = jnp.arange(plane_blocks, dtype=jnp.int32)
    run = blocks // RUN_BLOCKS
    offsets = jnp.asarray([-2, -1, 1, 2], jnp.int32)
    target = first + blocks[:, None] + offsets[None, :]
    reach = jnp.where(
        (run == (place + 3) % 4)[:, None],
        jnp.tile(before, 4)[:, None],
        jnp.tile(after, 4)[:, None],
    )
    window_live = (
        (jnp.abs(offsets)[None, :] <= reach)
        & (target >= 0)
        & (target < block_total)
        & (target // RUN_BLOCKS != (first + blocks)[:, None] // RUN_BLOCKS)
    )
    listed = lax.dynamic_slice_in_dim(rand_ids, first, plane_blocks, 0)
    globals_all = jnp.broadcast_to(global_ids[None, :], (plane_blocks, global_ids.shape[0]))
    slots = jnp.concatenate([target, globals_all, listed], axis=1)
    live = jnp.concatenate(
        [window_live, jnp.ones(globals_all.shape, jnp.bool_), listed >= 0], axis=1
    )
    held = live & ((slots >> 4) % 4 == place)
    return pack(held, (slots >> 6) * RUN_BLOCKS + (slots & (RUN_BLOCKS - 1)))


def per_device(tokens, query_weight, kv_weight, reach, global_ids, rand_ids):
    place = lax.axis_index("x").astype(jnp.int32)
    plane = (lax.axis_index("a") * 4 + lax.axis_index("b")).astype(jnp.int32)
    width = query_weight.shape[1]

    rows = lax.all_gather(tokens, ("y", "c"), axis=0, tiled=True)

    both = jnp.concatenate([kv_weight, query_weight], axis=1)
    both = lax.all_gather(both, "a", axis=0, tiled=True)
    kv_own = lax.all_gather(both[:, :width], "b", axis=0, tiled=True)
    query_own_in, kv_own = lax.optimization_barrier((both[:, width:], kv_own))

    def spread(own):
        own = own.reshape(4, 4, 64, width)
        return [own] + [shift(own, "x", s) for s in (1, 2, 3)]

    kv_parts = spread(kv_own)
    query_own = lax.all_gather(query_own_in, "b", axis=0, tiled=True)
    kv_parts, query_own = lax.optimization_barrier((kv_parts, query_own))

    place_1 = place.reshape(1)
    kv_rows = project(place_1, rows, kv_parts)
    held = lax.all_gather(kv_rows, ("a", "b"), axis=0, tiled=True)
    held = held.reshape(-1, BS, 2 * HD)
    query_own, reach, kv_rows = lax.optimization_barrier((query_own, reach, kv_rows))
    query_rows = project(place_1, rows, spread(query_own))
    queries = [query_rows] + [shift(query_rows, "x", s) for s in (1, 2, 3)]

    own_index, own_counts = own_lists(reach)
    zero = jnp.zeros((1,), jnp.int32)
    own_held = kv_rows.reshape(-1, BS, 2 * HD)
    [windows] = partial_attention(zero, own_index, own_counts, [query_rows], own_held)

    before, after = shift(reach, "x", 1), shift(reach, "x", 3)
    index, counts = plane_lists(before, after, global_ids, rand_ids, plane, place)
    held, windows, index, counts, queries = lax.optimization_barrier(
        (held, windows, index, counts, queries)
    )

    parts = [None] * 4
    for steps in ((2,), (1,), (3,), (0,)):
        from_x = jnp.stack([(place + 4 - k) % 4 for k in steps])
        mine = partial_attention(from_x, index, counts, [queries[k] for k in steps], held)
        for k, part in zip(steps, mine):
            parts[k] = part if k == 0 else shift(part, "x", 4 - k)
    return combine(parts + [windows])


def solution(mesh):
    inner = Mesh(mesh.devices.reshape(4, 4, 4, 4, 2), ("a", "b", "x", "y", "c"))
    ctx, tp = ("a", "b", "x"), ("y", "c")
    in_specs = (P(ctx + tp, None), P(ctx, tp), P(ctx, tp), P(ctx), P(), P())
    return jax.shard_map(
        per_device, mesh=inner, in_specs=in_specs, out_specs=P(ctx, tp), check_vma=False
    )
```

```python
import functools

import jax
import jax.numpy as jnp
from jax import lax
from jax.experimental import pallas as pl
from jax.experimental.pallas import tpu as pltpu
from jax.sharding import Mesh, PartitionSpec as P

HD = 128
BS = 64
WMAX = 2
CHUNK = 2
UNROLL = 8
SLOT_ROOM = 8
RUN_BLOCKS = 16
PAD = 32
ROW_TILE = 256
LOG2E = 1.4426950408889634
MASKED = -1e30
F32 = jnp.float32
BF16 = jnp.bfloat16
NT = (((1,), (1,)), ((), ()))
TN = (((0,), (0,)), ((), ()))


def shift(value, axis, by):
    size = lax.axis_size(axis)
    return lax.ppermute(value, axis, [(i, (i + by) % size) for i in range(size)])


def project_kernel(place, rows, part0, part1, part2, part3, out, buffer, weight, sems):
    count, depth = rows.shape

    def copy(t):
        tile = pl.ds(pl.multiple_of(t * ROW_TILE, ROW_TILE), ROW_TILE)
        return pltpu.make_async_copy(rows.at[tile], buffer.at[tile], sems.at[t])

    for t in range(count // ROW_TILE):
        copy(t).start()
    for s, part in enumerate((part0, part1, part2, part3)):
        owner = lax.rem(place[0] + 4 - s, 4)
        for za in range(4):
            for zb in range(4):
                weight[za * 4 + zb, owner] = part[zb, za]

    def step(t, carry):
        copy(t).wait()
        tile = pl.ds(pl.multiple_of(t * ROW_TILE, ROW_TILE), ROW_TILE)
        flat = weight[...].reshape(depth, out.shape[1])
        out[tile, :] = jnp.dot(
            buffer[tile, :], flat, preferred_element_type=F32
        ).astype(BF16)
        return carry

    lax.fori_loop(0, count // ROW_TILE, step, 0)


def project(place, rows, parts):
    count, depth = rows.shape
    width = parts[0].shape[-1]
    vmem = pl.BlockSpec(memory_space=pltpu.VMEM)
    return pl.pallas_call(
        project_kernel,
        in_specs=[pl.BlockSpec(memory_space=pltpu.SMEM), pl.BlockSpec(memory_space=pl.ANY)]
        + [vmem] * 4,
        out_specs=vmem,
        out_shape=jax.ShapeDtypeStruct((count, width), BF16),
        scratch_shapes=[
            pltpu.VMEM((count, depth), BF16),
            pltpu.VMEM((16, 4, 64, width), BF16),
            pltpu.SemaphoreType.DMA((count // ROW_TILE,)),
        ],
        compiler_params=pltpu.CompilerParams(vmem_limit_bytes=50 << 20),
        cost_estimate=pl.CostEstimate(
            flops=2 * count * depth * width,
            bytes_accessed=2 * (count * depth + depth * width + count * width),
            transcendentals=0,
        ),
        name="project",
    )(place, rows, *parts)


def partial_kernel(runs, from_x, index, counts, *refs):
    queries, held, outs = refs[:runs], refs[runs], refs[runs + 1 : 2 * runs + 1]
    slabs, near, far, sems, near_sems, far_sems = refs[-6:]

    def fetch(r):
        return pltpu.make_async_copy(queries[r], near.at[r], near_sems.at[r])

    def give(r):
        return pltpu.make_async_copy(far.at[r], outs[r], far_sems.at[r])

    for r in range(runs):
        fetch(r).start()

    def copy(r, j, p):
        row = (from_x[r] * RUN_BLOCKS + j) * SLOT_ROOM + p
        return pltpu.make_async_copy(
            held.at[index[row]],
            slabs.at[r * RUN_BLOCKS + j, pl.ds(p * BS, BS)],
            sems.at[r * RUN_BLOCKS + j, p],
        )

    def start_block(i, carry):
        r, j = i // RUN_BLOCKS, lax.rem(i, RUN_BLOCKS)

        def start(p, inner):
            copy(r, j, p).start()
            return inner

        return lax.fori_loop(0, counts[from_x[r] * RUN_BLOCKS + j], start, carry)

    lax.fori_loop(0, runs * RUN_BLOCKS, start_block, 0)

    for r in range(runs):
        fetch(r).wait()

    def run(r, carry):
        base = from_x[r] * RUN_BLOCKS
        attend_run(r, base, counts, copy, near.at[r], slabs, far.at[r])
        for fixed in range(runs):

            @pl.when(r == fixed)
            def _(fixed=fixed):
                give(fixed).start()

        return carry

    lax.fori_loop(0, runs, run, 0)
    for r in range(runs):
        give(r).wait()


def attend_run(r, base, counts, copy, query, slabs, out):
    def group(g, carry):
        first = g * UNROLL
        live = [counts[base + first + u] for u in range(UNROLL)]

        for u in range(UNROLL):

            def wait(p, inner, u=u):
                copy(r, first + u, p).wait()
                return inner

            lax.fori_loop(0, live[u], wait, 0)

        most = functools.reduce(jnp.maximum, live)
        row0 = g * (UNROLL * BS + PAD)

        def attend(chunks):
            keys = chunks * CHUNK * BS
            line = lax.broadcasted_iota(jnp.int32, (keys, HD), 0)
            spot = lax.broadcasted_iota(jnp.int32, (PAD, HD), 0)
            each = range(UNROLL)
            inside = [line < live[u] * BS for u in each]
            scores = []
            for u in each:
                q_rows = query[pl.ds((first + u) * BS, BS), :]
                q_both = jnp.concatenate([q_rows[:, :HD], q_rows[:, HD:]], axis=0)
                key = slabs[r * RUN_BLOCKS + first + u, 0:keys, 0:HD]
                scores.append(lax.dot_general(key, q_both, NT, preferred_element_type=F32))
            scores = [
                jnp.where(inside[u], scores[u] * (HD**-0.5 * LOG2E), MASKED) for u in each
            ]
            tops = [jnp.max(scores[u], axis=0, keepdims=True) for u in each]
            powers = [
                jnp.where(inside[u], jnp.exp2(scores[u] - tops[u]), 0.0) for u in each
            ]
            totals = [jnp.sum(powers[u], axis=0, keepdims=True) for u in each]
            some = [totals[u] > 0.0 for u in each]
            totals = [jnp.where(some[u], totals[u], 1.0) for u in each]
            weights = [(powers[u] * (1.0 / totals[u])).astype(BF16) for u in each]
            mixes = []
            for u in each:
                value = slabs[r * RUN_BLOCKS + first + u, 0:keys, HD : 2 * HD]
                value = jnp.where(inside[u], value, jnp.zeros_like(value))
                mixes.append(
                    lax.dot_general(weights[u], value, TN, preferred_element_type=F32)
                )
            stats = jnp.zeros((PAD, HD), F32)
            for u in each:
                level = jnp.where(some[u], tops[u] + jnp.log2(totals[u]), MASKED)
                high = level.astype(BF16).astype(F32)
                middle = (level - high).astype(BF16).astype(F32)
                for t, piece in enumerate((high, middle, level - high - middle)):
                    stats = jnp.where(spot == 3 * u + t, piece, stats)
            for u in each:
                mixed = mixes[u].astype(BF16)
                out[pl.ds(row0 + u * BS, BS), 0:HD] = mixed[:BS]
                out[pl.ds(row0 + u * BS, BS), HD : 2 * HD] = mixed[BS:]
            out[pl.ds(row0 + UNROLL * BS, PAD), 0:HD] = stats.astype(BF16)
            out[pl.ds(row0 + UNROLL * BS, PAD), HD : 2 * HD] = jnp.zeros((PAD, HD), BF16)

        for chunks in (1, 2, 3, 4):
            low_edge = (chunks - 1) * CHUNK if chunks > 1 else -1

            @pl.when((most > low_edge) & (most <= chunks * CHUNK))
            def _(chunks=chunks):
                attend(chunks)

        return carry

    lax.fori_loop(0, RUN_BLOCKS // UNROLL, group, 0)


def partial_attention(from_x, index, counts, queries, held):
    runs = len(queries)
    rows = RUN_BLOCKS // UNROLL * (UNROLL * BS + PAD)
    smem = pl.BlockSpec(memory_space=pltpu.SMEM)
    return pl.pallas_call(
        functools.partial(partial_kernel, runs),
        in_specs=[smem] * 3 + [pl.BlockSpec(memory_space=pl.ANY)] * (runs + 1),
        out_specs=[pl.BlockSpec(memory_space=pl.ANY)] * runs,
        out_shape=[jax.ShapeDtypeStruct((rows, 2 * HD), BF16)] * runs,
        scratch_shapes=[
            pltpu.VMEM((runs * RUN_BLOCKS, SLOT_ROOM * BS, 2 * HD), BF16),
            pltpu.VMEM((runs, RUN_BLOCKS * BS, 2 * HD), BF16),
            pltpu.VMEM((runs, rows, 2 * HD), BF16),
            pltpu.SemaphoreType.DMA((runs * RUN_BLOCKS, SLOT_ROOM)),
            pltpu.SemaphoreType.DMA((runs,)),
            pltpu.SemaphoreType.DMA((runs,)),
        ],
        compiler_params=pltpu.CompilerParams(vmem_limit_bytes=50 << 20),
        cost_estimate=pl.CostEstimate(
            flops=runs * 5 * 10**9, bytes_accessed=4 << 20, transcendentals=0
        ),
        name="partial_attention",
    )(from_x, index, counts, *queries, held)


def combine_kernel(*refs):
    parts, out = refs[:-1], refs[-1]
    spot = lax.broadcasted_iota(jnp.int32, (HD, HD), 0)

    def group(g, carry):
        row0 = g * (UNROLL * BS + PAD)
        tail = [p[pl.ds(row0 + UNROLL * BS, PAD), 0:HD].astype(F32) for p in parts]
        tables = []
        for u in range(UNROLL):
            levels = [
                t[3 * u : 3 * u + 1] + t[3 * u + 1 : 3 * u + 2] + t[3 * u + 2 : 3 * u + 3]
                for t in tail
            ]
            top = functools.reduce(jnp.maximum, levels)
            shares = [jnp.exp2(level - top) for level in levels]
            norm = 1.0 / functools.reduce(jnp.add, shares)
            table = jnp.zeros((HD, HD), F32)
            for k, share in enumerate(shares):
                table = jnp.where(spot == k, share * norm, table)
            tables.append(table.T)
        for u in range(UNROLL):
            for h in range(2):
                lanes = slice(h * HD, (h + 1) * HD)
                mixed = jnp.zeros((BS, HD), F32)
                for k, part in enumerate(parts):
                    scale = tables[u][h * BS : (h + 1) * BS, k : k + 1]
                    mixed += scale * part[pl.ds(row0 + u * BS, BS), lanes].astype(F32)
                out[pl.ds((g * UNROLL + u) * BS, BS), lanes] = mixed.astype(BF16)
        return carry

    lax.fori_loop(0, RUN_BLOCKS // UNROLL, group, 0)


def combine(parts):
    vmem = pl.BlockSpec(memory_space=pltpu.VMEM)
    return pl.pallas_call(
        combine_kernel,
        in_specs=[vmem] * len(parts),
        out_specs=vmem,
        out_shape=jax.ShapeDtypeStruct((RUN_BLOCKS * BS, 2 * HD), BF16),
        compiler_params=pltpu.CompilerParams(vmem_limit_bytes=16 << 20),
        name="combine",
    )(*parts)


def pack(held, local):
    slots = held.shape[1]
    source, target = jnp.arange(slots), jnp.arange(SLOT_ROOM)
    before = source[:, None] < source[None, :]
    rank = jnp.sum(jnp.where(held[:, :, None] & before[None], 1, 0), axis=1)
    at = held[:, :, None] & (rank[:, :, None] == target[None, None, :])
    index = jnp.sum(jnp.where(at, local[:, :, None], 0), axis=1)
    counts = jnp.sum(held.astype(jnp.int32), axis=1)
    return index.reshape(-1).astype(jnp.int32), counts.astype(jnp.int32)


def own_lists(reach):
    offsets = jnp.arange(-WMAX, WMAX + 1, dtype=jnp.int32)
    target = jnp.arange(RUN_BLOCKS, dtype=jnp.int32)[:, None] + offsets[None, :]
    live = (
        (jnp.abs(offsets)[None, :] <= reach[:, None]) & (target >= 0) & (target < RUN_BLOCKS)
    )
    return pack(live, target)


def plane_lists(before, after, global_ids, rand_ids, plane, place):
    plane_blocks = 4 * RUN_BLOCKS
    block_total = rand_ids.shape[0]
    first = plane * plane_blocks
    blocks = jnp.arange(plane_blocks, dtype=jnp.int32)
    run = blocks // RUN_BLOCKS
    offsets = jnp.asarray([-2, -1, 1, 2], jnp.int32)
    target = first + blocks[:, None] + offsets[None, :]
    reach = jnp.where(
        (run == (place + 3) % 4)[:, None],
        jnp.tile(before, 4)[:, None],
        jnp.tile(after, 4)[:, None],
    )
    window_live = (
        (jnp.abs(offsets)[None, :] <= reach)
        & (target >= 0)
        & (target < block_total)
        & (target // RUN_BLOCKS != (first + blocks)[:, None] // RUN_BLOCKS)
    )
    listed = lax.dynamic_slice_in_dim(rand_ids, first, plane_blocks, 0)
    globals_all = jnp.broadcast_to(global_ids[None, :], (plane_blocks, global_ids.shape[0]))
    slots = jnp.concatenate([target, globals_all, listed], axis=1)
    live = jnp.concatenate(
        [window_live, jnp.ones(globals_all.shape, jnp.bool_), listed >= 0], axis=1
    )
    held = live & ((slots >> 4) % 4 == place)
    return pack(held, (slots >> 6) * RUN_BLOCKS + (slots & (RUN_BLOCKS - 1)))


def per_device(tokens, query_weight, kv_weight, reach, global_ids, rand_ids):
    place = lax.axis_index("x").astype(jnp.int32)
    plane = (lax.axis_index("a") * 4 + lax.axis_index("b")).astype(jnp.int32)
    width = query_weight.shape[1]

    rows = lax.all_gather(tokens, ("y", "c"), axis=0, tiled=True)

    both = jnp.concatenate([kv_weight, query_weight], axis=1)
    both = lax.all_gather(both, "a", axis=0, tiled=True)
    kv_own = lax.all_gather(both[:, :width], "b", axis=0, tiled=True)
    query_own_in, kv_own = lax.optimization_barrier((both[:, width:], kv_own))

    def spread(own):
        own = own.reshape(4, 4, 64, width)
        return [own] + [shift(own, "x", s) for s in (1, 2, 3)]

    kv_parts = spread(kv_own)
    query_own = lax.all_gather(query_own_in, "b", axis=0, tiled=True)
    kv_parts, query_own = lax.optimization_barrier((kv_parts, query_own))

    place_1 = place.reshape(1)
    kv_rows = project(place_1, rows, kv_parts)
    held = lax.all_gather(kv_rows, ("a", "b"), axis=0, tiled=True)
    held = held.reshape(-1, BS, 2 * HD)
    query_own, reach, kv_rows = lax.optimization_barrier((query_own, reach, kv_rows))
    query_rows = project(place_1, rows, spread(query_own))
    queries = [query_rows] + [shift(query_rows, "x", s) for s in (1, 2, 3)]

    own_index, own_counts = own_lists(reach)
    zero = jnp.zeros((1,), jnp.int32)
    own_held = kv_rows.reshape(-1, BS, 2 * HD)
    [windows] = partial_attention(zero, own_index, own_counts, [query_rows], own_held)

    before, after = shift(reach, "x", 1), shift(reach, "x", 3)
    index, counts = plane_lists(before, after, global_ids, rand_ids, plane, place)
    held, windows, index, counts, queries = lax.optimization_barrier(
        (held, windows, index, counts, queries)
    )

    parts = [None] * 4
    for steps in ((2, 1, 3), (0,)):
        from_x = jnp.stack([(place + 4 - k) % 4 for k in steps])
        mine = partial_attention(from_x, index, counts, [queries[k] for k in steps], held)
        for k, part in zip(steps, mine):
            parts[k] = part if k == 0 else shift(part, "x", 4 - k)
    return combine(parts + [windows])


def solution(mesh):
    inner = Mesh(mesh.devices.reshape(4, 4, 4, 4, 2), ("a", "b", "x", "y", "c"))
    ctx, tp = ("a", "b", "x"), ("y", "c")
    in_specs = (P(ctx + tp, None), P(ctx, tp), P(ctx, tp), P(ctx), P(), P())
    return jax.shard_map(
        per_device, mesh=inner, in_specs=in_specs, out_specs=P(ctx, tp), check_vma=False
    )
```

```python
import functools

import jax
import jax.numpy as jnp
from jax import lax
from jax.experimental import pallas as pl
from jax.experimental.pallas import tpu as pltpu
from jax.sharding import Mesh, PartitionSpec as P

HD = 128
BS = 64
WMAX = 2
CHUNK = 2
UNROLL = 8
SLOT_ROOM = 8
RUN_BLOCKS = 16
PAD = 64
ROW_TILE = 256
LOG2E = 1.4426950408889634
MASKED = -1e30
F32 = jnp.float32
BF16 = jnp.bfloat16
NT = (((1,), (1,)), ((), ()))


def shift(value, axis, by):
    size = lax.axis_size(axis)
    return lax.ppermute(value, axis, [(i, (i + by) % size) for i in range(size)])


def project_kernel(place, rows, part0, part1, part2, part3, out, buffer, weight, sems):
    count, depth = rows.shape

    def copy(t):
        tile = pl.ds(pl.multiple_of(t * ROW_TILE, ROW_TILE), ROW_TILE)
        return pltpu.make_async_copy(rows.at[tile], buffer.at[tile], sems.at[t])

    for t in range(count // ROW_TILE):
        copy(t).start()
    for s, part in enumerate((part0, part1, part2, part3)):
        owner = lax.rem(place[0] + 4 - s, 4)
        for za in range(4):
            for zb in range(4):
                weight[za * 4 + zb, owner] = part[zb, za]

    def step(t, carry):
        copy(t).wait()
        tile = pl.ds(pl.multiple_of(t * ROW_TILE, ROW_TILE), ROW_TILE)
        flat = weight[...].reshape(depth, out.shape[1])
        out[tile, :] = jnp.dot(
            buffer[tile, :], flat, preferred_element_type=F32
        ).astype(BF16)
        return carry

    lax.fori_loop(0, count // ROW_TILE, step, 0)


def project(place, rows, parts):
    count, depth = rows.shape
    width = parts[0].shape[-1]
    vmem = pl.BlockSpec(memory_space=pltpu.VMEM)
    return pl.pallas_call(
        project_kernel,
        in_specs=[pl.BlockSpec(memory_space=pltpu.SMEM), pl.BlockSpec(memory_space=pl.ANY)]
        + [vmem] * 4,
        out_specs=vmem,
        out_shape=jax.ShapeDtypeStruct((count, width), BF16),
        scratch_shapes=[
            pltpu.VMEM((count, depth), BF16),
            pltpu.VMEM((16, 4, 64, width), BF16),
            pltpu.SemaphoreType.DMA((count // ROW_TILE,)),
        ],
        compiler_params=pltpu.CompilerParams(vmem_limit_bytes=50 << 20),
        cost_estimate=pl.CostEstimate(
            flops=2 * count * depth * width,
            bytes_accessed=2 * (count * depth + depth * width + count * width),
            transcendentals=0,
        ),
        name="project",
    )(place, rows, *parts)


def partial_kernel(from_x, index, counts, query, held, out, slabs, tops_at, sums_at, sems):
    base = from_x[0] * RUN_BLOCKS

    def copy(j, p):
        return pltpu.make_async_copy(
            held.at[index[(base + j) * SLOT_ROOM + p]],
            slabs.at[j, pl.ds(p * BS, BS)],
            sems.at[j, p],
        )

    def start_block(j, carry):
        def start(p, inner):
            copy(j, p).start()
            return inner

        return lax.fori_loop(0, counts[base + j], start, carry)

    lax.fori_loop(0, RUN_BLOCKS, start_block, 0)

    def group(g, carry):
        first = g * UNROLL
        live = [counts[base + first + u] for u in range(UNROLL)]

        for u in range(UNROLL):

            def wait(p, inner, u=u):
                copy(first + u, p).wait()
                return inner

            lax.fori_loop(0, live[u], wait, 0)

        most = functools.reduce(jnp.maximum, live)

        def attend(chunks):
            keys = chunks * CHUNK * BS
            each = range(UNROLL)
            lane = lax.broadcasted_iota(jnp.int32, (2 * BS, keys), 1)
            line = lax.broadcasted_iota(jnp.int32, (keys, HD), 0)
            spot = lax.broadcasted_iota(jnp.int32, (2 * BS, HD), 1)
            ones = jnp.ones((keys, HD), BF16)
            scores = []
            for u in each:
                q_rows = query[pl.ds((first + u) * BS, BS), :]
                q_both = jnp.concatenate([q_rows[:, :HD], q_rows[:, HD:]], axis=0)
                key = slabs[first + u, 0:keys, 0:HD]
                scores.append(lax.dot_general(q_both, key, NT, preferred_element_type=F32))
            scores = [
                jnp.where(lane < live[u] * BS, scores[u] * (HD**-0.5 * LOG2E), MASKED)
                for u in each
            ]
            tops = [jnp.max(scores[u], axis=1, keepdims=True) for u in each]
            powers = [jnp.exp2(scores[u] - tops[u]).astype(BF16) for u in each]
            mixes = []
            for u in each:
                value = slabs[first + u, 0:keys, HD : 2 * HD]
                value = jnp.where(line < live[u] * BS, value, jnp.zeros_like(value))
                value = jnp.concatenate([value, ones], axis=1)
                mixes.append(jnp.dot(powers[u], value, preferred_element_type=F32))
            top_table, sum_table = tops_at[...], sums_at[...]
            for u in each:
                here = spot == first + u
                top_table = jnp.where(here, tops[u], top_table)
                sum_table = jnp.where(here, mixes[u][:, HD:], sum_table)
            tops_at[...], sums_at[...] = top_table, sum_table
            for u in each:
                mixed = (mixes[u][:, :HD] * (1.0 / mixes[u][:, HD:])).astype(BF16)
                out[pl.ds((first + u) * BS, BS), 0:HD] = mixed[:BS]
                out[pl.ds((first + u) * BS, BS), HD : 2 * HD] = mixed[BS:]

        for chunks in (1, 2, 3, 4):
            low_edge = (chunks - 1) * CHUNK if chunks > 1 else -1

            @pl.when((most > low_edge) & (most <= chunks * CHUNK))
            def _(chunks=chunks):
                attend(chunks)

        return carry

    tops_at[...] = jnp.zeros_like(tops_at)
    sums_at[...] = jnp.ones_like(sums_at)
    lax.fori_loop(0, RUN_BLOCKS // UNROLL, group, 0)
    spot = lax.broadcasted_iota(jnp.int32, (2 * BS, HD), 1)
    level = jnp.where(spot < RUN_BLOCKS, tops_at[...] + jnp.log2(sums_at[...]), 0.0)
    high = level.astype(BF16).astype(F32)
    middle = (level - high).astype(BF16).astype(F32)
    low = level - high - middle
    packed = (
        high + pltpu.roll(middle, RUN_BLOCKS, 1) + pltpu.roll(low, 2 * RUN_BLOCKS, 1)
    ).astype(BF16)
    out[pl.ds(RUN_BLOCKS * BS, PAD), 0:HD] = packed[:BS]
    out[pl.ds(RUN_BLOCKS * BS, PAD), HD : 2 * HD] = packed[BS:]


def partial_attention(from_x, index, counts, query, held):
    rows = RUN_BLOCKS * BS + PAD
    smem = pl.BlockSpec(memory_space=pltpu.SMEM)
    vmem = pl.BlockSpec(memory_space=pltpu.VMEM)
    return pl.pallas_call(
        partial_kernel,
        in_specs=[smem] * 3 + [vmem, pl.BlockSpec(memory_space=pl.ANY)],
        out_specs=vmem,
        out_shape=jax.ShapeDtypeStruct((rows, 2 * HD), BF16),
        scratch_shapes=[
            pltpu.VMEM((RUN_BLOCKS, SLOT_ROOM * BS, 2 * HD), BF16),
            pltpu.VMEM((2 * BS, HD), F32),
            pltpu.VMEM((2 * BS, HD), F32),
            pltpu.SemaphoreType.DMA((RUN_BLOCKS, SLOT_ROOM)),
        ],
        compiler_params=pltpu.CompilerParams(vmem_limit_bytes=50 << 20),
        cost_estimate=pl.CostEstimate(
            flops=2 * 10**9, bytes_accessed=1 << 16, transcendentals=0
        ),
        name="partial_attention",
    )(from_x, index, counts, query, held)


def combine_kernel(*refs):
    parts, out = refs[:-1], refs[-1]
    rows = pl.ds(RUN_BLOCKS * BS, PAD)
    scales = []
    for h in range(2):
        lanes = slice(h * HD, (h + 1) * HD)
        levels = []
        for part in parts:
            packed = part[rows, lanes].astype(F32)
            levels.append(
                packed
                + pltpu.roll(packed, HD - RUN_BLOCKS, 1)
                + pltpu.roll(packed, HD - 2 * RUN_BLOCKS, 1)
            )
        top = functools.reduce(jnp.maximum, levels)
        shares = [jnp.exp2(level - top) for level in levels]
        norm = 1.0 / functools.reduce(jnp.add, shares)
        scales.append([share * norm for share in shares])
    for j in range(RUN_BLOCKS):
        block = slice(j * BS, (j + 1) * BS)
        for h in range(2):
            lanes = slice(h * HD, (h + 1) * HD)
            terms = [
                scales[h][k][:, j : j + 1] * part[block, lanes].astype(F32)
                for k, part in enumerate(parts)
            ]
            out[block, lanes] = functools.reduce(jnp.add, terms).astype(BF16)


def combine(parts):
    vmem = pl.BlockSpec(memory_space=pltpu.VMEM)
    return pl.pallas_call(
        combine_kernel,
        in_specs=[vmem] * len(parts),
        out_specs=vmem,
        out_shape=jax.ShapeDtypeStruct((RUN_BLOCKS * BS, 2 * HD), BF16),
        compiler_params=pltpu.CompilerParams(vmem_limit_bytes=16 << 20),
        name="combine",
    )(*parts)


def pack(held, local):
    slots = held.shape[1]
    source, target = jnp.arange(slots), jnp.arange(SLOT_ROOM)
    before = source[:, None] < source[None, :]
    rank = jnp.sum(jnp.where(held[:, :, None] & before[None], 1, 0), axis=1)
    at = held[:, :, None] & (rank[:, :, None] == target[None, None, :])
    index = jnp.sum(jnp.where(at, local[:, :, None], 0), axis=1)
    counts = jnp.sum(held.astype(jnp.int32), axis=1)
    return index.reshape(-1).astype(jnp.int32), counts.astype(jnp.int32)


def own_lists(reach):
    offsets = jnp.arange(-WMAX, WMAX + 1, dtype=jnp.int32)
    target = jnp.arange(RUN_BLOCKS, dtype=jnp.int32)[:, None] + offsets[None, :]
    live = (
        (jnp.abs(offsets)[None, :] <= reach[:, None]) & (target >= 0) & (target < RUN_BLOCKS)
    )
    return pack(live, target)


def plane_lists(before, after, global_ids, rand_ids, plane, place):
    plane_blocks = 4 * RUN_BLOCKS
    block_total = rand_ids.shape[0]
    first = plane * plane_blocks
    blocks = jnp.arange(plane_blocks, dtype=jnp.int32)
    run = blocks // RUN_BLOCKS
    offsets = jnp.asarray([-2, -1, 1, 2], jnp.int32)
    target = first + blocks[:, None] + offsets[None, :]
    reach = jnp.where(
        (run == (place + 3) % 4)[:, None],
        jnp.tile(before, 4)[:, None],
        jnp.tile(after, 4)[:, None],
    )
    window_live = (
        (jnp.abs(offsets)[None, :] <= reach)
        & (target >= 0)
        & (target < block_total)
        & (target // RUN_BLOCKS != (first + blocks)[:, None] // RUN_BLOCKS)
    )
    listed = lax.dynamic_slice_in_dim(rand_ids, first, plane_blocks, 0)
    globals_all = jnp.broadcast_to(global_ids[None, :], (plane_blocks, global_ids.shape[0]))
    slots = jnp.concatenate([target, globals_all, listed], axis=1)
    live = jnp.concatenate(
        [window_live, jnp.ones(globals_all.shape, jnp.bool_), listed >= 0], axis=1
    )
    held = live & ((slots >> 4) % 4 == place)
    return pack(held, (slots >> 6) * RUN_BLOCKS + (slots & (RUN_BLOCKS - 1)))


def per_device(tokens, query_weight, kv_weight, reach, global_ids, rand_ids):
    place = lax.axis_index("x").astype(jnp.int32)
    plane = (lax.axis_index("a") * 4 + lax.axis_index("b")).astype(jnp.int32)
    width = query_weight.shape[1]

    rows = lax.all_gather(tokens, ("y", "c"), axis=0, tiled=True)

    both = jnp.concatenate([kv_weight, query_weight], axis=1)
    both = lax.all_gather(both, "a", axis=0, tiled=True)
    kv_own = lax.all_gather(both[:, :width], "b", axis=0, tiled=True)
    query_own_in, kv_own = lax.optimization_barrier((both[:, width:], kv_own))

    def spread(own):
        own = own.reshape(4, 4, 64, width)
        return [own] + [shift(own, "x", s) for s in (1, 2, 3)]

    kv_parts = spread(kv_own)
    query_own = lax.all_gather(query_own_in, "b", axis=0, tiled=True)
    kv_parts, query_own = lax.optimization_barrier((kv_parts, query_own))

    place_1 = place.reshape(1)
    kv_rows = project(place_1, rows, kv_parts)
    held = lax.all_gather(kv_rows, ("a", "b"), axis=0, tiled=True)
    held = held.reshape(-1, BS, 2 * HD)
    query_own, reach, kv_rows = lax.optimization_barrier((query_own, reach, kv_rows))
    query_rows = project(place_1, rows, spread(query_own))
    queries = [query_rows] + [shift(query_rows, "x", s) for s in (1, 2, 3)]

    own_index, own_counts = own_lists(reach)
    zero = jnp.zeros((1,), jnp.int32)
    own_held = kv_rows.reshape(-1, BS, 2 * HD)
    windows = partial_attention(zero, own_index, own_counts, query_rows, own_held)

    before, after = shift(reach, "x", 1), shift(reach, "x", 3)
    index, counts = plane_lists(before, after, global_ids, rand_ids, plane, place)
    held, windows, index, counts, queries = lax.optimization_barrier(
        (held, windows, index, counts, queries)
    )

    parts = [None] * 4
    turn = place
    for s in (2, 1, 3, 0):
        from_x = ((turn + 4 - s) % 4).reshape(1)
        part = partial_attention(from_x, index, counts, queries[s], held)
        parts[s] = part if s == 0 else shift(part, "x", 4 - s)
    return combine([parts[0], parts[3], parts[1], parts[2], windows])


def solution(mesh):
    inner = Mesh(mesh.devices.reshape(4, 4, 4, 4, 2), ("a", "b", "x", "y", "c"))
    ctx, tp = ("a", "b", "x"), ("y", "c")
    in_specs = (P(ctx + tp, None), P(ctx, tp), P(ctx, tp), P(ctx), P(), P())
    return jax.shard_map(
        per_device, mesh=inner, in_specs=in_specs, out_specs=P(ctx, tp), check_vma=False
    )
```

```python
import functools

import jax
import jax.numpy as jnp
from jax import lax
from jax.experimental import pallas as pl
from jax.experimental.pallas import tpu as pltpu
from jax.sharding import Mesh, PartitionSpec as P

HD = 128
BS = 64
WMAX = 2
CHUNK = 2
UNROLL = 8
SLOT_ROOM = 8
RUN_BLOCKS = 16
PAD = 64
ROW_TILE = 256
ORDER = (0, 2, 1, 3)
LOG2E = 1.4426950408889634
MASKED = -1e30
F32 = jnp.float32
BF16 = jnp.bfloat16
NT = (((1,), (1,)), ((), ()))


def shift(value, axis, by):
    size = lax.axis_size(axis)
    return lax.ppermute(value, axis, [(i, (i + by) % size) for i in range(size)])


def project_kernel(place, rows, part0, part1, part2, part3, out, buffer, weight, sems):
    count, depth = rows.shape

    def copy(t):
        tile = pl.ds(pl.multiple_of(t * ROW_TILE, ROW_TILE), ROW_TILE)
        return pltpu.make_async_copy(rows.at[tile], buffer.at[tile], sems.at[t])

    for t in range(count // ROW_TILE):
        copy(t).start()
    for s, part in zip(ORDER, (part0, part1, part2, part3)):
        owner = lax.rem(place[0] + 4 - s, 4)
        for za in range(4):
            for zb in range(4):
                weight[za * 4 + zb, owner] = part[zb, za]

    def step(t, carry):
        copy(t).wait()
        tile = pl.ds(pl.multiple_of(t * ROW_TILE, ROW_TILE), ROW_TILE)
        flat = weight[...].reshape(depth, out.shape[1])
        out[tile, :] = jnp.dot(
            buffer[tile, :], flat, preferred_element_type=F32
        ).astype(BF16)
        return carry

    lax.fori_loop(0, count // ROW_TILE, step, 0)


def project(place, rows, parts):
    count, depth = rows.shape
    width = parts[0].shape[-1]
    vmem = pl.BlockSpec(memory_space=pltpu.VMEM)
    return pl.pallas_call(
        project_kernel,
        in_specs=[pl.BlockSpec(memory_space=pltpu.SMEM), pl.BlockSpec(memory_space=pl.ANY)]
        + [vmem] * 4,
        out_specs=vmem,
        out_shape=jax.ShapeDtypeStruct((count, width), BF16),
        scratch_shapes=[
            pltpu.VMEM((count, depth), BF16),
            pltpu.VMEM((16, 4, 64, width), BF16),
            pltpu.SemaphoreType.DMA((count // ROW_TILE,)),
        ],
        compiler_params=pltpu.CompilerParams(vmem_limit_bytes=50 << 20),
        cost_estimate=pl.CostEstimate(
            flops=2 * count * depth * width,
            bytes_accessed=2 * (count * depth + depth * width + count * width),
            transcendentals=0,
        ),
        name="project",
    )(place, rows, *parts)


def partial_kernel(from_x, index, counts, query, held, out, slabs, tops_at, sums_at, sems):
    base = from_x[0] * RUN_BLOCKS

    def copy(j, p):
        return pltpu.make_async_copy(
            held.at[index[(base + j) * SLOT_ROOM + p]],
            slabs.at[j, pl.ds(p * BS, BS)],
            sems.at[j, p],
        )

    def start_block(j, carry):
        def start(p, inner):
            copy(j, p).start()
            return inner

        return lax.fori_loop(0, counts[base + j], start, carry)

    lax.fori_loop(0, RUN_BLOCKS, start_block, 0)

    def group(g, carry):
        first = g * UNROLL
        live = [counts[base + first + u] for u in range(UNROLL)]

        for u in range(UNROLL):

            def wait(p, inner, u=u):
                copy(first + u, p).wait()
                return inner

            lax.fori_loop(0, live[u], wait, 0)

        most = functools.reduce(jnp.maximum, live)

        def attend(chunks):
            keys = chunks * CHUNK * BS
            each = range(UNROLL)
            lane = lax.broadcasted_iota(jnp.int32, (2 * BS, keys), 1)
            line = lax.broadcasted_iota(jnp.int32, (keys, HD), 0)
            spot = lax.broadcasted_iota(jnp.int32, (2 * BS, HD), 1)
            ones = jnp.ones((keys, HD), BF16)
            scores = []
            for u in each:
                q_rows = query[pl.ds((first + u) * BS, BS), :]
                q_both = jnp.concatenate([q_rows[:, :HD], q_rows[:, HD:]], axis=0)
                key = slabs[first + u, 0:keys, 0:HD]
                scores.append(lax.dot_general(q_both, key, NT, preferred_element_type=F32))
            scores = [
                jnp.where(lane < live[u] * BS, scores[u] * (HD**-0.5 * LOG2E), MASKED)
                for u in each
            ]
            tops = [jnp.max(scores[u], axis=1, keepdims=True) for u in each]
            powers = [jnp.exp2(scores[u] - tops[u]).astype(BF16) for u in each]
            mixes = []
            for u in each:
                value = slabs[first + u, 0:keys, HD : 2 * HD]
                value = jnp.where(line < live[u] * BS, value, jnp.zeros_like(value))
                value = jnp.concatenate([value, ones], axis=1)
                mixes.append(jnp.dot(powers[u], value, preferred_element_type=F32))
            top_table, sum_table = tops_at[...], sums_at[...]
            for u in each:
                here = spot == first + u
                top_table = jnp.where(here, tops[u], top_table)
                sum_table = jnp.where(here, mixes[u][:, HD:], sum_table)
            tops_at[...], sums_at[...] = top_table, sum_table
            for u in each:
                mixed = (mixes[u][:, :HD] * (1.0 / mixes[u][:, HD:])).astype(BF16)
                out[pl.ds((first + u) * BS, BS), 0:HD] = mixed[:BS]
                out[pl.ds((first + u) * BS, BS), HD : 2 * HD] = mixed[BS:]

        for chunks in (1, 2, 3, 4):
            low_edge = (chunks - 1) * CHUNK if chunks > 1 else -1

            @pl.when((most > low_edge) & (most <= chunks * CHUNK))
            def _(chunks=chunks):
                attend(chunks)

        return carry

    tops_at[...] = jnp.zeros_like(tops_at)
    sums_at[...] = jnp.ones_like(sums_at)
    lax.fori_loop(0, RUN_BLOCKS // UNROLL, group, 0)
    spot = lax.broadcasted_iota(jnp.int32, (2 * BS, HD), 1)
    level = jnp.where(spot < RUN_BLOCKS, tops_at[...] + jnp.log2(sums_at[...]), 0.0)
    high = level.astype(BF16).astype(F32)
    middle = (level - high).astype(BF16).astype(F32)
    low = level - high - middle
    packed = (
        high + pltpu.roll(middle, RUN_BLOCKS, 1) + pltpu.roll(low, 2 * RUN_BLOCKS, 1)
    ).astype(BF16)
    out[pl.ds(RUN_BLOCKS * BS, PAD), 0:HD] = packed[:BS]
    out[pl.ds(RUN_BLOCKS * BS, PAD), HD : 2 * HD] = packed[BS:]


def partial_attention(from_x, index, counts, query, held):
    rows = RUN_BLOCKS * BS + PAD
    smem = pl.BlockSpec(memory_space=pltpu.SMEM)
    vmem = pl.BlockSpec(memory_space=pltpu.VMEM)
    return pl.pallas_call(
        partial_kernel,
        in_specs=[smem] * 3 + [vmem, pl.BlockSpec(memory_space=pl.ANY)],
        out_specs=vmem,
        out_shape=jax.ShapeDtypeStruct((rows, 2 * HD), BF16),
        scratch_shapes=[
            pltpu.VMEM((RUN_BLOCKS, SLOT_ROOM * BS, 2 * HD), BF16),
            pltpu.VMEM((2 * BS, HD), F32),
            pltpu.VMEM((2 * BS, HD), F32),
            pltpu.SemaphoreType.DMA((RUN_BLOCKS, SLOT_ROOM)),
        ],
        compiler_params=pltpu.CompilerParams(vmem_limit_bytes=50 << 20),
        cost_estimate=pl.CostEstimate(
            flops=2 * 10**9, bytes_accessed=1 << 16, transcendentals=0
        ),
        name="partial_attention",
    )(from_x, index, counts, query, held)


def combine_kernel(*refs):
    parts, out = refs[:-1], refs[-1]
    rows = pl.ds(RUN_BLOCKS * BS, PAD)
    scales = []
    for h in range(2):
        lanes = slice(h * HD, (h + 1) * HD)
        levels = []
        for part in parts:
            packed = part[rows, lanes].astype(F32)
            levels.append(
                packed
                + pltpu.roll(packed, HD - RUN_BLOCKS, 1)
                + pltpu.roll(packed, HD - 2 * RUN_BLOCKS, 1)
            )
        top = functools.reduce(jnp.maximum, levels)
        shares = [jnp.exp2(level - top) for level in levels]
        norm = 1.0 / functools.reduce(jnp.add, shares)
        scales.append([share * norm for share in shares])
    for j in range(RUN_BLOCKS):
        block = slice(j * BS, (j + 1) * BS)
        for h in range(2):
            lanes = slice(h * HD, (h + 1) * HD)
            terms = [
                scales[h][k][:, j : j + 1] * part[block, lanes].astype(F32)
                for k, part in enumerate(parts)
            ]
            out[block, lanes] = functools.reduce(jnp.add, terms).astype(BF16)


def combine(parts):
    vmem = pl.BlockSpec(memory_space=pltpu.VMEM)
    return pl.pallas_call(
        combine_kernel,
        in_specs=[vmem] * len(parts),
        out_specs=vmem,
        out_shape=jax.ShapeDtypeStruct((RUN_BLOCKS * BS, 2 * HD), BF16),
        compiler_params=pltpu.CompilerParams(vmem_limit_bytes=16 << 20),
        name="combine",
    )(*parts)


def pack(held, local):
    slots = held.shape[1]
    source, target = jnp.arange(slots), jnp.arange(SLOT_ROOM)
    before = source[:, None] < source[None, :]
    rank = jnp.sum(jnp.where(held[:, :, None] & before[None], 1, 0), axis=1)
    at = held[:, :, None] & (rank[:, :, None] == target[None, None, :])
    index = jnp.sum(jnp.where(at, local[:, :, None], 0), axis=1)
    counts = jnp.sum(held.astype(jnp.int32), axis=1)
    return index.reshape(-1).astype(jnp.int32), counts.astype(jnp.int32)


def own_lists(reach):
    offsets = jnp.arange(-WMAX, WMAX + 1, dtype=jnp.int32)
    target = jnp.arange(RUN_BLOCKS, dtype=jnp.int32)[:, None] + offsets[None, :]
    live = (
        (jnp.abs(offsets)[None, :] <= reach[:, None]) & (target >= 0) & (target < RUN_BLOCKS)
    )
    return pack(live, target)


def plane_lists(before, after, global_ids, rand_ids, plane, place):
    plane_blocks = 4 * RUN_BLOCKS
    block_total = rand_ids.shape[0]
    first = plane * plane_blocks
    blocks = jnp.arange(plane_blocks, dtype=jnp.int32)
    run = blocks // RUN_BLOCKS
    offsets = jnp.asarray([-2, -1, 1, 2], jnp.int32)
    target = first + blocks[:, None] + offsets[None, :]
    reach = jnp.where(
        (run == (place + 3) % 4)[:, None],
        jnp.tile(before, 4)[:, None],
        jnp.tile(after, 4)[:, None],
    )
    window_live = (
        (jnp.abs(offsets)[None, :] <= reach)
        & (target >= 0)
        & (target < block_total)
        & (target // RUN_BLOCKS != (first + blocks)[:, None] // RUN_BLOCKS)
    )
    listed = lax.dynamic_slice_in_dim(rand_ids, first, plane_blocks, 0)
    globals_all = jnp.broadcast_to(global_ids[None, :], (plane_blocks, global_ids.shape[0]))
    slots = jnp.concatenate([target, globals_all, listed], axis=1)
    live = jnp.concatenate(
        [window_live, jnp.ones(globals_all.shape, jnp.bool_), listed >= 0], axis=1
    )
    held = live & ((slots >> 4) % 4 == place)
    return pack(held, (slots >> 6) * RUN_BLOCKS + (slots & (RUN_BLOCKS - 1)))


def per_device(tokens, query_weight, kv_weight, reach, global_ids, rand_ids):
    place = lax.axis_index("x").astype(jnp.int32)
    plane = (lax.axis_index("a") * 4 + lax.axis_index("b")).astype(jnp.int32)
    width = query_weight.shape[1]

    rows = lax.all_gather(tokens, ("y", "c"), axis=0, tiled=True)

    kv_own = lax.all_gather(kv_weight, "a", axis=0, tiled=True)
    kv_own = lax.all_gather(kv_own, "b", axis=0, tiled=True)
    query_weight, kv_own = lax.optimization_barrier((query_weight, kv_own))

    def spread(own):
        own = own.reshape(4, 4, 64, width)
        return [shift(own, "x", s) if s else own for s in ORDER]

    kv_parts = spread(kv_own)
    query_own = lax.all_gather(query_weight, "a", axis=0, tiled=True)
    kv_parts, query_own = lax.optimization_barrier((kv_parts, query_own))

    place_1 = place.reshape(1)
    kv_rows = project(place_1, rows, kv_parts)
    held = lax.all_gather(kv_rows, ("a", "b"), axis=0, tiled=True)
    held = held.reshape(-1, BS, 2 * HD)
    query_own, reach, kv_rows = lax.optimization_barrier((query_own, reach, kv_rows))
    query_own = lax.all_gather(query_own, "b", axis=0, tiled=True)
    query_rows = project(place_1, rows, spread(query_own))
    queries = [query_rows] + [shift(query_rows, "x", s) for s in (1, 2, 3)]

    own_index, own_counts = own_lists(reach)
    zero = jnp.zeros((1,), jnp.int32)
    own_held = kv_rows.reshape(-1, BS, 2 * HD)
    windows = partial_attention(zero, own_index, own_counts, query_rows, own_held)

    before, after = shift(reach, "x", 1), shift(reach, "x", 3)
    index, counts = plane_lists(before, after, global_ids, rand_ids, plane, place)
    held, windows, index, counts, queries = lax.optimization_barrier(
        (held, windows, index, counts, queries)
    )

    parts = [None] * 4
    turn = place
    for s in (2, 1, 3, 0):
        from_x = ((turn + 4 - s) % 4).reshape(1)
        part = partial_attention(from_x, index, counts, queries[s], held)
        parts[s] = part if s == 0 else shift(part, "x", 4 - s)
    return combine([parts[0], parts[3], parts[1], parts[2], windows])


def solution(mesh):
    inner = Mesh(mesh.devices.reshape(4, 4, 4, 4, 2), ("a", "b", "x", "y", "c"))
    ctx, tp = ("a", "b", "x"), ("y", "c")
    in_specs = (P(ctx + tp, None), P(ctx, tp), P(ctx, tp), P(ctx), P(), P())
    return jax.shard_map(
        per_device, mesh=inner, in_specs=in_specs, out_specs=P(ctx, tp), check_vma=False
    )
```

```python
import functools

import jax
import jax.numpy as jnp
from jax import lax
from jax.experimental import pallas as pl
from jax.experimental.pallas import tpu as pltpu
from jax.sharding import Mesh, PartitionSpec as P

HD = 128
BS = 64
WMAX = 2
CHUNK = 2
UNROLL = 8
SLOT_ROOM = 8
RUN_BLOCKS = 16
PAD = 64
ROW_TILE = 256
LOG2E = 1.4426950408889634
MASKED = -1e30
F32 = jnp.float32
BF16 = jnp.bfloat16
NT = (((1,), (1,)), ((), ()))


def shift(value, axis, by):
    size = lax.axis_size(axis)
    return lax.ppermute(value, axis, [(i, (i + by) % size) for i in range(size)])


def project_kernel(ring, place, rows, part0, part1, part2, part3, out, buffer, weight, sems):
    count, depth = rows.shape

    def copy(t):
        tile = pl.ds(pl.multiple_of(t * ROW_TILE, ROW_TILE), ROW_TILE)
        return pltpu.make_async_copy(rows.at[tile], buffer.at[tile], sems.at[t])

    for t in range(count // ROW_TILE):
        copy(t).start()
    for s, part in enumerate((part0, part1, part2, part3)):
        owner = lax.rem(place[0] + 4 - s, 4)
        for za in range(4):
            for zb in range(4):
                at = lax.rem(place[1] + 4 - zb, 4) if ring else zb
                weight[za * 4 + at, owner] = part[zb, za]

    def step(t, carry):
        copy(t).wait()
        tile = pl.ds(pl.multiple_of(t * ROW_TILE, ROW_TILE), ROW_TILE)
        flat = weight[...].reshape(depth, out.shape[1])
        out[tile, :] = jnp.dot(
            buffer[tile, :], flat, preferred_element_type=F32
        ).astype(BF16)
        return carry

    lax.fori_loop(0, count // ROW_TILE, step, 0)


def project(ring, place, rows, parts):
    count, depth = rows.shape
    width = parts[0].shape[-1]
    vmem = pl.BlockSpec(memory_space=pltpu.VMEM)
    return pl.pallas_call(
        functools.partial(project_kernel, ring),
        in_specs=[pl.BlockSpec(memory_space=pltpu.SMEM), pl.BlockSpec(memory_space=pl.ANY)]
        + [vmem] * 4,
        out_specs=vmem,
        out_shape=jax.ShapeDtypeStruct((count, width), BF16),
        scratch_shapes=[
            pltpu.VMEM((count, depth), BF16),
            pltpu.VMEM((16, 4, 64, width), BF16),
            pltpu.SemaphoreType.DMA((count // ROW_TILE,)),
        ],
        compiler_params=pltpu.CompilerParams(vmem_limit_bytes=50 << 20),
        cost_estimate=pl.CostEstimate(
            flops=2 * count * depth * width,
            bytes_accessed=2 * (count * depth + depth * width + count * width),
            transcendentals=0,
        ),
        name="project",
    )(place, rows, *parts)


def partial_kernel(from_x, index, counts, query, held, out, slabs, tops_at, sums_at, sems):
    base = from_x[0] * RUN_BLOCKS

    def copy(j, p):
        return pltpu.make_async_copy(
            held.at[index[(base + j) * SLOT_ROOM + p]],
            slabs.at[j, pl.ds(p * BS, BS)],
            sems.at[j, p],
        )

    def start_block(j, carry):
        def start(p, inner):
            copy(j, p).start()
            return inner

        return lax.fori_loop(0, counts[base + j], start, carry)

    lax.fori_loop(0, RUN_BLOCKS, start_block, 0)

    def group(g, carry):
        first = g * UNROLL
        live = [counts[base + first + u] for u in range(UNROLL)]

        for u in range(UNROLL):

            def wait(p, inner, u=u):
                copy(first + u, p).wait()
                return inner

            lax.fori_loop(0, live[u], wait, 0)

        most = functools.reduce(jnp.maximum, live)

        def attend(chunks):
            keys = chunks * CHUNK * BS
            each = range(UNROLL)
            lane = lax.broadcasted_iota(jnp.int32, (2 * BS, keys), 1)
            line = lax.broadcasted_iota(jnp.int32, (keys, HD), 0)
            spot = lax.broadcasted_iota(jnp.int32, (2 * BS, HD), 1)
            ones = jnp.ones((keys, HD), BF16)
            scores = []
            for u in each:
                q_rows = query[pl.ds((first + u) * BS, BS), :]
                q_both = jnp.concatenate([q_rows[:, :HD], q_rows[:, HD:]], axis=0)
                key = slabs[first + u, 0:keys, 0:HD]
                scores.append(lax.dot_general(q_both, key, NT, preferred_element_type=F32))
            scores = [
                jnp.where(lane < live[u] * BS, scores[u] * (HD**-0.5 * LOG2E), MASKED)
                for u in each
            ]
            tops = [jnp.max(scores[u], axis=1, keepdims=True) for u in each]
            powers = [jnp.exp2(scores[u] - tops[u]).astype(BF16) for u in each]
            mixes = []
            for u in each:
                value = slabs[first + u, 0:keys, HD : 2 * HD]
                value = jnp.where(line < live[u] * BS, value, jnp.zeros_like(value))
                value = jnp.concatenate([value, ones], axis=1)
                mixes.append(jnp.dot(powers[u], value, preferred_element_type=F32))
            top_table, sum_table = tops_at[...], sums_at[...]
            for u in each:
                here = spot == first + u
                top_table = jnp.where(here, tops[u], top_table)
                sum_table = jnp.where(here, mixes[u][:, HD:], sum_table)
            tops_at[...], sums_at[...] = top_table, sum_table
            for u in each:
                mixed = (mixes[u][:, :HD] * (1.0 / mixes[u][:, HD:])).astype(BF16)
                out[pl.ds((first + u) * BS, BS), 0:HD] = mixed[:BS]
                out[pl.ds((first + u) * BS, BS), HD : 2 * HD] = mixed[BS:]

        for chunks in (1, 2, 3, 4):
            low_edge = (chunks - 1) * CHUNK if chunks > 1 else -1

            @pl.when((most > low_edge) & (most <= chunks * CHUNK))
            def _(chunks=chunks):
                attend(chunks)

        return carry

    tops_at[...] = jnp.zeros_like(tops_at)
    sums_at[...] = jnp.ones_like(sums_at)
    lax.fori_loop(0, RUN_BLOCKS // UNROLL, group, 0)
    spot = lax.broadcasted_iota(jnp.int32, (2 * BS, HD), 1)
    level = jnp.where(spot < RUN_BLOCKS, tops_at[...] + jnp.log2(sums_at[...]), 0.0)
    high = level.astype(BF16).astype(F32)
    middle = (level - high).astype(BF16).astype(F32)
    low = level - high - middle
    packed = (
        high + pltpu.roll(middle, RUN_BLOCKS, 1) + pltpu.roll(low, 2 * RUN_BLOCKS, 1)
    ).astype(BF16)
    out[pl.ds(RUN_BLOCKS * BS, PAD), 0:HD] = packed[:BS]
    out[pl.ds(RUN_BLOCKS * BS, PAD), HD : 2 * HD] = packed[BS:]


def partial_attention(from_x, index, counts, query, held):
    rows = RUN_BLOCKS * BS + PAD
    smem = pl.BlockSpec(memory_space=pltpu.SMEM)
    vmem = pl.BlockSpec(memory_space=pltpu.VMEM)
    return pl.pallas_call(
        partial_kernel,
        in_specs=[smem] * 3 + [vmem, pl.BlockSpec(memory_space=pl.ANY)],
        out_specs=vmem,
        out_shape=jax.ShapeDtypeStruct((rows, 2 * HD), BF16),
        scratch_shapes=[
            pltpu.VMEM((RUN_BLOCKS, SLOT_ROOM * BS, 2 * HD), BF16),
            pltpu.VMEM((2 * BS, HD), F32),
            pltpu.VMEM((2 * BS, HD), F32),
            pltpu.SemaphoreType.DMA((RUN_BLOCKS, SLOT_ROOM)),
        ],
        compiler_params=pltpu.CompilerParams(vmem_limit_bytes=50 << 20),
        cost_estimate=pl.CostEstimate(
            flops=2 * 10**9, bytes_accessed=1 << 16, transcendentals=0
        ),
        name="partial_attention",
    )(from_x, index, counts, query, held)


def combine_kernel(*refs):
    parts, out = refs[:-1], refs[-1]
    rows = pl.ds(RUN_BLOCKS * BS, PAD)
    scales = []
    for h in range(2):
        lanes = slice(h * HD, (h + 1) * HD)
        levels = []
        for part in parts:
            packed = part[rows, lanes].astype(F32)
            levels.append(
                packed
                + pltpu.roll(packed, HD - RUN_BLOCKS, 1)
                + pltpu.roll(packed, HD - 2 * RUN_BLOCKS, 1)
            )
        top = functools.reduce(jnp.maximum, levels)
        shares = [jnp.exp2(level - top) for level in levels]
        norm = 1.0 / functools.reduce(jnp.add, shares)
        scales.append([share * norm for share in shares])
    for j in range(RUN_BLOCKS):
        block = slice(j * BS, (j + 1) * BS)
        for h in range(2):
            lanes = slice(h * HD, (h + 1) * HD)
            terms = [
                scales[h][k][:, j : j + 1] * part[block, lanes].astype(F32)
                for k, part in enumerate(parts)
            ]
            out[block, lanes] = functools.reduce(jnp.add, terms).astype(BF16)


def combine(parts):
    vmem = pl.BlockSpec(memory_space=pltpu.VMEM)
    return pl.pallas_call(
        combine_kernel,
        in_specs=[vmem] * len(parts),
        out_specs=vmem,
        out_shape=jax.ShapeDtypeStruct((RUN_BLOCKS * BS, 2 * HD), BF16),
        compiler_params=pltpu.CompilerParams(vmem_limit_bytes=16 << 20),
        name="combine",
    )(*parts)


def pack(held, local):
    slots = held.shape[1]
    source, target = jnp.arange(slots), jnp.arange(SLOT_ROOM)
    before = source[:, None] < source[None, :]
    rank = jnp.sum(jnp.where(held[:, :, None] & before[None], 1, 0), axis=1)
    at = held[:, :, None] & (rank[:, :, None] == target[None, None, :])
    index = jnp.sum(jnp.where(at, local[:, :, None], 0), axis=1)
    counts = jnp.sum(held.astype(jnp.int32), axis=1)
    return index.reshape(-1).astype(jnp.int32), counts.astype(jnp.int32)


def own_lists(reach):
    offsets = jnp.arange(-WMAX, WMAX + 1, dtype=jnp.int32)
    target = jnp.arange(RUN_BLOCKS, dtype=jnp.int32)[:, None] + offsets[None, :]
    live = (
        (jnp.abs(offsets)[None, :] <= reach[:, None]) & (target >= 0) & (target < RUN_BLOCKS)
    )
    return pack(live, target)


def plane_lists(before, after, global_ids, rand_ids, plane, place):
    plane_blocks = 4 * RUN_BLOCKS
    block_total = rand_ids.shape[0]
    first = plane * plane_blocks
    blocks = jnp.arange(plane_blocks, dtype=jnp.int32)
    run = blocks // RUN_BLOCKS
    offsets = jnp.asarray([-2, -1, 1, 2], jnp.int32)
    target = first + blocks[:, None] + offsets[None, :]
    reach = jnp.where(
        (run == (place + 3) % 4)[:, None],
        jnp.tile(before, 4)[:, None],
        jnp.tile(after, 4)[:, None],
    )
    window_live = (
        (jnp.abs(offsets)[None, :] <= reach)
        & (target >= 0)
        & (target < block_total)
        & (target // RUN_BLOCKS != (first + blocks)[:, None] // RUN_BLOCKS)
    )
    listed = lax.dynamic_slice_in_dim(rand_ids, first, plane_blocks, 0)
    globals_all = jnp.broadcast_to(global_ids[None, :], (plane_blocks, global_ids.shape[0]))
    slots = jnp.concatenate([target, globals_all, listed], axis=1)
    live = jnp.concatenate(
        [window_live, jnp.ones(globals_all.shape, jnp.bool_), listed >= 0], axis=1
    )
    held = live & ((slots >> 4) % 4 == place)
    return pack(held, (slots >> 6) * RUN_BLOCKS + (slots & (RUN_BLOCKS - 1)))


def per_device(tokens, query_weight, kv_weight, reach, global_ids, rand_ids):
    place = lax.axis_index("x").astype(jnp.int32)
    plane = (lax.axis_index("a") * 4 + lax.axis_index("b")).astype(jnp.int32)
    width = query_weight.shape[1]

    rows = lax.all_gather(tokens, ("y", "c"), axis=0, tiled=True)

    both = jnp.concatenate([kv_weight, query_weight], axis=1)
    both = lax.all_gather(both, "a", axis=0, tiled=True)
    kv_own = lax.all_gather(both[:, :width], "b", axis=0, tiled=True)
    query_first, kv_own = lax.optimization_barrier((both[:, width:], kv_own))

    def spread(own):
        own = own.reshape(4, 4, 64, width)
        return [own] + [shift(own, "x", s) for s in (1, 2, 3)]

    kv_parts = spread(kv_own)
    planes = 16
    query_turns = [query_first] + [
        lax.ppermute(query_first, ("a", "b"), [(i, (i + t) % planes) for i in range(planes)])
        for t in (1, 2, planes - 1)
    ]

    place_2 = jnp.stack([place, lax.axis_index("b").astype(jnp.int32)])
    kv_rows = project(False, place_2, rows, kv_parts)
    held = lax.all_gather(kv_rows, ("a", "b"), axis=0, tiled=True)
    held = held.reshape(-1, BS, 2 * HD)
    query_turns, reach, kv_rows = lax.optimization_barrier((query_turns, reach, kv_rows))
    query_rows = project(True, place_2, rows, spread(jnp.stack(query_turns)))
    queries = [query_rows] + [shift(query_rows, "x", s) for s in (1, 2, 3)]

    own_index, own_counts = own_lists(reach)
    zero = jnp.zeros((1,), jnp.int32)
    own_held = kv_rows.reshape(-1, BS, 2 * HD)
    windows = partial_attention(zero, own_index, own_counts, query_rows, own_held)

    before, after = shift(reach, "x", 1), shift(reach, "x", 3)
    index, counts = plane_lists(before, after, global_ids, rand_ids, plane, place)
    held, windows, index, counts, queries = lax.optimization_barrier(
        (held, windows, index, counts, queries)
    )

    parts = [None] * 4
    turn = place
    for s in (2, 1, 3, 0):
        from_x = ((turn + 4 - s) % 4).reshape(1)
        part = partial_attention(from_x, index, counts, queries[s], held)
        parts[s] = part if s == 0 else shift(part, "x", 4 - s)
    return combine([parts[0], parts[3], parts[1], parts[2], windows])


def solution(mesh):
    inner = Mesh(mesh.devices.reshape(4, 4, 4, 4, 2), ("a", "b", "x", "y", "c"))
    ctx, tp = ("a", "b", "x"), ("y", "c")
    in_specs = (P(ctx + tp, None), P(ctx, tp), P(ctx, tp), P(ctx), P(), P())
    return jax.shard_map(
        per_device, mesh=inner, in_specs=in_specs, out_specs=P(ctx, tp), check_vma=False
    )
```

```python
import functools

import jax
import jax.numpy as jnp
from jax import lax
from jax.experimental import pallas as pl
from jax.experimental.pallas import tpu as pltpu
from jax.sharding import Mesh, PartitionSpec as P

HD = 128
BS = 64
WMAX = 2
CHUNK = 2
UNROLL = 8
SLOT_ROOM = 8
RUN_BLOCKS = 16
PAD = 64
ROW_TILE = 256
LOG2E = 1.4426950408889634
MASKED = -1e30
F32 = jnp.float32
BF16 = jnp.bfloat16
NT = (((1,), (1,)), ((), ()))


def shift(value, axis, by):
    size = lax.axis_size(axis)
    return lax.ppermute(value, axis, [(i, (i + by) % size) for i in range(size)])


def project_kernel(place, rows, part0, part1, part2, part3, out, buffer, weight, sems):
    count, depth = rows.shape

    def copy(t):
        tile = pl.ds(pl.multiple_of(t * ROW_TILE, ROW_TILE), ROW_TILE)
        return pltpu.make_async_copy(rows.at[tile], buffer.at[tile], sems.at[t])

    for t in range(count // ROW_TILE):
        copy(t).start()
    for s, part in enumerate((part0, part1, part2, part3)):
        owner = lax.rem(place[0] + 4 - s, 4)
        for za in range(4):
            for zb in range(4):
                weight[za * 4 + zb, owner] = part[zb, za]

    def step(t, carry):
        copy(t).wait()
        tile = pl.ds(pl.multiple_of(t * ROW_TILE, ROW_TILE), ROW_TILE)
        flat = weight[...].reshape(depth, out.shape[1])
        out[tile, :] = jnp.dot(
            buffer[tile, :], flat, preferred_element_type=F32
        ).astype(BF16)
        return carry

    lax.fori_loop(0, count // ROW_TILE, step, 0)


def project(place, rows, parts):
    count, depth = rows.shape
    width = parts[0].shape[-1]
    vmem = pl.BlockSpec(memory_space=pltpu.VMEM)
    return pl.pallas_call(
        project_kernel,
        in_specs=[pl.BlockSpec(memory_space=pltpu.SMEM), pl.BlockSpec(memory_space=pl.ANY)]
        + [vmem] * 4,
        out_specs=vmem,
        out_shape=jax.ShapeDtypeStruct((count, width), BF16),
        scratch_shapes=[
            pltpu.VMEM((count, depth), BF16),
            pltpu.VMEM((16, 4, 64, width), BF16),
            pltpu.SemaphoreType.DMA((count // ROW_TILE,)),
        ],
        compiler_params=pltpu.CompilerParams(vmem_limit_bytes=50 << 20),
        cost_estimate=pl.CostEstimate(
            flops=2 * count * depth * width,
            bytes_accessed=2 * (count * depth + depth * width + count * width),
            transcendentals=0,
        ),
        name="project",
    )(place, rows, *parts)


def terms_of(level):
    level = jnp.where(lax.broadcasted_iota(jnp.int32, level.shape, 1) < RUN_BLOCKS, level, 0.0)
    high = level.astype(BF16).astype(F32)
    middle = (level - high).astype(BF16).astype(F32)
    low = level - high - middle
    return (
        high + pltpu.roll(middle, RUN_BLOCKS, 1) + pltpu.roll(low, 2 * RUN_BLOCKS, 1)
    ).astype(BF16)


def partial_kernel(from_x, index, counts, query, held, out, slabs, tops_at, sums_at, sems):
    base = from_x[0] * RUN_BLOCKS

    def copy(j, p):
        return pltpu.make_async_copy(
            held.at[index[(base + j) * SLOT_ROOM + p]],
            slabs.at[j, pl.ds(p * BS, BS)],
            sems.at[j, p],
        )

    def start_block(j, carry):
        def start(p, inner):
            copy(j, p).start()
            return inner

        return lax.fori_loop(0, counts[base + j], start, carry)

    lax.fori_loop(0, RUN_BLOCKS, start_block, 0)

    def group(g, carry):
        first = g * UNROLL
        live = [counts[base + first + u] for u in range(UNROLL)]

        for u in range(UNROLL):

            def wait(p, inner, u=u):
                copy(first + u, p).wait()
                return inner

            lax.fori_loop(0, live[u], wait, 0)

        most = functools.reduce(jnp.maximum, live)

        def attend(chunks):
            keys = chunks * CHUNK * BS
            each = range(UNROLL)
            lane = lax.broadcasted_iota(jnp.int32, (2 * BS, keys), 1)
            line = lax.broadcasted_iota(jnp.int32, (keys, HD), 0)
            spot = lax.broadcasted_iota(jnp.int32, (2 * BS, HD), 1)
            ones = jnp.ones((keys, HD), BF16)
            scores = []
            for u in each:
                q_rows = query[pl.ds((first + u) * BS, BS), :]
                q_both = jnp.concatenate([q_rows[:, :HD], q_rows[:, HD:]], axis=0)
                key = slabs[first + u, 0:keys, 0:HD]
                scores.append(lax.dot_general(q_both, key, NT, preferred_element_type=F32))
            scores = [
                jnp.where(lane < live[u] * BS, scores[u] * (HD**-0.5 * LOG2E), MASKED)
                for u in each
            ]
            tops = [jnp.max(scores[u], axis=1, keepdims=True) for u in each]
            powers = [jnp.exp2(scores[u] - tops[u]).astype(BF16) for u in each]
            mixes = []
            for u in each:
                value = slabs[first + u, 0:keys, HD : 2 * HD]
                value = jnp.where(line < live[u] * BS, value, jnp.zeros_like(value))
                value = jnp.concatenate([value, ones], axis=1)
                mixes.append(jnp.dot(powers[u], value, preferred_element_type=F32))
            top_table, sum_table = tops_at[...], sums_at[...]
            for u in each:
                here = spot == first + u
                top_table = jnp.where(here, tops[u], top_table)
                sum_table = jnp.where(here, mixes[u][:, HD:], sum_table)
            tops_at[...], sums_at[...] = top_table, sum_table
            for u in each:
                mixed = (mixes[u][:, :HD] * (1.0 / mixes[u][:, HD:])).astype(BF16)
                out[pl.ds((first + u) * BS, BS), 0:HD] = mixed[:BS]
                out[pl.ds((first + u) * BS, BS), HD : 2 * HD] = mixed[BS:]

        for chunks in (1, 2, 3, 4):
            low_edge = (chunks - 1) * CHUNK if chunks > 1 else -1

            @pl.when((most > low_edge) & (most <= chunks * CHUNK))
            def _(chunks=chunks):
                attend(chunks)

        return carry

    tops_at[...] = jnp.zeros_like(tops_at)
    sums_at[...] = jnp.ones_like(sums_at)
    lax.fori_loop(0, RUN_BLOCKS // UNROLL, group, 0)
    packed = terms_of(tops_at[...] + jnp.log2(sums_at[...]))
    out[pl.ds(RUN_BLOCKS * BS, PAD), 0:HD] = packed[:BS]
    out[pl.ds(RUN_BLOCKS * BS, PAD), HD : 2 * HD] = packed[BS:]


def partial_attention(from_x, index, counts, query, held):
    rows = RUN_BLOCKS * BS + PAD
    smem = pl.BlockSpec(memory_space=pltpu.SMEM)
    vmem = pl.BlockSpec(memory_space=pltpu.VMEM)
    return pl.pallas_call(
        partial_kernel,
        in_specs=[smem] * 3 + [vmem, pl.BlockSpec(memory_space=pl.ANY)],
        out_specs=vmem,
        out_shape=jax.ShapeDtypeStruct((rows, 2 * HD), BF16),
        scratch_shapes=[
            pltpu.VMEM((RUN_BLOCKS, SLOT_ROOM * BS, 2 * HD), BF16),
            pltpu.VMEM((2 * BS, HD), F32),
            pltpu.VMEM((2 * BS, HD), F32),
            pltpu.SemaphoreType.DMA((RUN_BLOCKS, SLOT_ROOM)),
        ],
        compiler_params=pltpu.CompilerParams(vmem_limit_bytes=50 << 20),
        cost_estimate=pl.CostEstimate(
            flops=2 * 10**9, bytes_accessed=1 << 16, transcendentals=0
        ),
        name="partial_attention",
    )(from_x, index, counts, query, held)


def combine_kernel(keep, *refs):
    parts, out = refs[:-1], refs[-1]
    rows = pl.ds(RUN_BLOCKS * BS, PAD)
    scales = []
    for h in range(2):
        lanes = slice(h * HD, (h + 1) * HD)
        levels = []
        for part in parts:
            packed = part[rows, lanes].astype(F32)
            levels.append(
                packed
                + pltpu.roll(packed, HD - RUN_BLOCKS, 1)
                + pltpu.roll(packed, HD - 2 * RUN_BLOCKS, 1)
            )
        top = functools.reduce(jnp.maximum, levels)
        shares = [jnp.exp2(level - top) for level in levels]
        total = functools.reduce(jnp.add, shares)
        norm = 1.0 / total
        if keep:
            out[rows, lanes] = terms_of(top + jnp.log2(total))
        scales.append([share * norm for share in shares])
    for j in range(RUN_BLOCKS):
        block = slice(j * BS, (j + 1) * BS)
        for h in range(2):
            lanes = slice(h * HD, (h + 1) * HD)
            terms = [
                scales[h][k][:, j : j + 1] * part[block, lanes].astype(F32)
                for k, part in enumerate(parts)
            ]
            out[block, lanes] = functools.reduce(jnp.add, terms).astype(BF16)


def combine(parts, keep=False):
    vmem = pl.BlockSpec(memory_space=pltpu.VMEM)
    return pl.pallas_call(
        functools.partial(combine_kernel, keep),
        in_specs=[vmem] * len(parts),
        out_specs=vmem,
        out_shape=jax.ShapeDtypeStruct((RUN_BLOCKS * BS + keep * PAD, 2 * HD), BF16),
        compiler_params=pltpu.CompilerParams(vmem_limit_bytes=16 << 20),
        name="combine",
    )(*parts)


def pack(held, local):
    slots = held.shape[1]
    source, target = jnp.arange(slots), jnp.arange(SLOT_ROOM)
    before = source[:, None] < source[None, :]
    rank = jnp.sum(jnp.where(held[:, :, None] & before[None], 1, 0), axis=1)
    at = held[:, :, None] & (rank[:, :, None] == target[None, None, :])
    index = jnp.sum(jnp.where(at, local[:, :, None], 0), axis=1)
    counts = jnp.sum(held.astype(jnp.int32), axis=1)
    return index.reshape(-1).astype(jnp.int32), counts.astype(jnp.int32)


def own_lists(reach):
    offsets = jnp.arange(-WMAX, WMAX + 1, dtype=jnp.int32)
    target = jnp.arange(RUN_BLOCKS, dtype=jnp.int32)[:, None] + offsets[None, :]
    live = (
        (jnp.abs(offsets)[None, :] <= reach[:, None]) & (target >= 0) & (target < RUN_BLOCKS)
    )
    return pack(live, target)


def plane_lists(before, after, global_ids, rand_ids, plane, place):
    plane_blocks = 4 * RUN_BLOCKS
    block_total = rand_ids.shape[0]
    first = plane * plane_blocks
    blocks = jnp.arange(plane_blocks, dtype=jnp.int32)
    run = blocks // RUN_BLOCKS
    offsets = jnp.asarray([-2, -1, 1, 2], jnp.int32)
    target = first + blocks[:, None] + offsets[None, :]
    reach = jnp.where(
        (run == (place + 3) % 4)[:, None],
        jnp.tile(before, 4)[:, None],
        jnp.tile(after, 4)[:, None],
    )
    window_live = (
        (jnp.abs(offsets)[None, :] <= reach)
        & (target >= 0)
        & (target < block_total)
        & (target // RUN_BLOCKS != (first + blocks)[:, None] // RUN_BLOCKS)
    )
    listed = lax.dynamic_slice_in_dim(rand_ids, first, plane_blocks, 0)
    globals_all = jnp.broadcast_to(global_ids[None, :], (plane_blocks, global_ids.shape[0]))
    slots = jnp.concatenate([target, globals_all, listed], axis=1)
    live = jnp.concatenate(
        [window_live, jnp.ones(globals_all.shape, jnp.bool_), listed >= 0], axis=1
    )
    held = live & ((slots >> 4) % 4 == place)
    return pack(held, (slots >> 6) * RUN_BLOCKS + (slots & (RUN_BLOCKS - 1)))


def per_device(tokens, query_weight, kv_weight, reach, global_ids, rand_ids):
    place = lax.axis_index("x").astype(jnp.int32)
    plane = (lax.axis_index("a") * 4 + lax.axis_index("b")).astype(jnp.int32)
    width = query_weight.shape[1]

    rows = lax.all_gather(tokens, ("y", "c"), axis=0, tiled=True)

    both = jnp.concatenate([kv_weight, query_weight], axis=1)
    both = lax.all_gather(both, "a", axis=0, tiled=True)
    kv_own = lax.all_gather(both[:, :width], "b", axis=0, tiled=True)
    query_own_in, kv_own = lax.optimization_barrier((both[:, width:], kv_own))

    def spread(own):
        own = own.reshape(4, 4, 64, width)
        return [own] + [shift(own, "x", s) for s in (1, 2, 3)]

    kv_parts = spread(kv_own)
    query_own = lax.all_gather(query_own_in, "b", axis=0, tiled=True)
    kv_parts, query_own = lax.optimization_barrier((kv_parts, query_own))

    place_1 = place.reshape(1)
    kv_rows = project(place_1, rows, kv_parts)
    held = lax.all_gather(kv_rows, ("a", "b"), axis=0, tiled=True)
    held = held.reshape(-1, BS, 2 * HD)
    query_own, reach, kv_rows = lax.optimization_barrier((query_own, reach, kv_rows))
    query_rows = project(place_1, rows, spread(query_own))
    queries = [query_rows] + [shift(query_rows, "x", s) for s in (1, 2, 3)]

    own_index, own_counts = own_lists(reach)
    zero = jnp.zeros((1,), jnp.int32)
    own_held = kv_rows.reshape(-1, BS, 2 * HD)
    windows = partial_attention(zero, own_index, own_counts, query_rows, own_held)

    before, after = shift(reach, "x", 1), shift(reach, "x", 3)
    index, counts = plane_lists(before, after, global_ids, rand_ids, plane, place)
    held, windows, index, counts, queries = lax.optimization_barrier(
        (held, windows, index, counts, queries)
    )

    parts = [None] * 4
    turn = place
    for s in (2, 1, 3, 0):
        from_x = ((turn + 4 - s) % 4).reshape(1)
        part = partial_attention(from_x, index, counts, queries[s], held)
        parts[s] = part if s == 0 else shift(part, "x", 4 - s)
    most = combine([parts[0], parts[1], parts[2], windows], keep=True)
    return combine([most, parts[3]])


def solution(mesh):
    inner = Mesh(mesh.devices.reshape(4, 4, 4, 4, 2), ("a", "b", "x", "y", "c"))
    ctx, tp = ("a", "b", "x"), ("y", "c")
    in_specs = (P(ctx + tp, None), P(ctx, tp), P(ctx, tp), P(ctx), P(), P())
    return jax.shard_map(
        per_device, mesh=inner, in_specs=in_specs, out_specs=P(ctx, tp), check_vma=False
    )
```
